32 devices in a mesh: dp: 4 (over x, core), ctx: 8 (over z, y).
Axes of the slice: x: 2, y: 2, z: 4, core: 2. Of those that a mesh axis runs over, the one named last changes fastest.
Arguments:
- query_proj: bfloat16 [4, 1024, 4096], P('dp', 'ctx'), may hold values from -6 to 6
- key_proj: bfloat16 [4, 1024, 4096], P('dp', 'ctx'), may hold values from -6 to 6
- value_proj: bfloat16 [4, 1024, 4096], P('dp', 'ctx'), may hold values from -6 to 6
- doc_offset: int32 [4, 1024], P('dp', 'ctx'), may hold values from 0 to 1023, as said below
- short_taps: float32 [3, 7, 4096], replicated, may hold values from -2.5 to 2.5
- rate_scale: float32 [16, 4096], replicated, may hold values from 0.1 to 120
- residue: float32 [16, 4096], replicated, may hold values from -2.5 to 2.5
- skip_gain: float32 [4096], replicated, may hold values from 0.5 to 1.5
- out_grad: bfloat16 [4, 1024, 4096], P('dp', 'ctx'), may hold values from -6 to 6
Outputs:
- mixed_out: bfloat16 [4, 1024, 4096], P('dp', 'ctx')
- query_grad: bfloat16 [4, 1024, 4096], P('dp', 'ctx')
- key_grad: bfloat16 [4, 1024, 4096], P('dp', 'ctx')
- value_grad: bfloat16 [4, 1024, 4096], P('dp', 'ctx')
- taps_grad: float32 [3, 7, 4096], replicated
- skip_grad: float32 [4096], replicated
- residue_grad: float32 [16, 4096], replicated
The draws below stay inside these ranges and needn't reach their ends.
Inputs may be any that keep to these rules, and one draw needn't show every extreme that they name: `doc_offset`: each row is a run of whole documents: the value is a token's index inside its document, 0 at a document's first position and rising by one along it. The first row holds a single document.
All inputs are finite; a program needn't handle non-finite values.
Results may differ from the reference program's by a relative error of at most 0.0013.
Values may be sent and summed in bfloat16 or wider, within the bound.
A program may use at most 192 MiB of HBM per device.

```python
import math
import jax
import jax.numpy as jnp
from jax import lax

CH = 4096
ORDER = 16
TAPS = 7
SEQ = 1024
ROWS = 4


def draw_doc_offset(key, part):
    starts = jax.random.randint(key, (ROWS, SEQ), 0, SEQ) < 4
    positions = jnp.broadcast_to(jnp.arange(SEQ, dtype=jnp.int32)[None, :], (ROWS, SEQ))
    single_doc = jnp.arange(ROWS, dtype=jnp.int32)[:, None] == 0
    starts = jnp.logical_and(starts, jnp.logical_not(single_doc))
    starts = jnp.logical_or(starts, positions == 0)
    last_start = lax.cummax(jnp.where(starts, positions, 0), axis=1)
    return (positions - last_start).astype(jnp.int32)


def shard_levels(rng, dims, cuts, low, top_value):
    loudness, own = 1.0, jax.random.fold_in(rng, 6)
    for axis_at, blocks in cuts:
        draws = jnp.exp(jax.random.uniform(jax.random.fold_in(own, axis_at), (blocks,), jnp.float32, low / len(cuts), top_value / len(cuts)))
        loudness = loudness * jnp.repeat(draws, dims[axis_at] // blocks).reshape([-1 if axis == axis_at else 1 for axis in range(len(dims))])
    return loudness


def normal_values(key, dims, width, bound, split=(), held_as=jnp.bfloat16):
    result = jax.random.normal(key, dims, jnp.float32) * width
    if len(split) > 0:
        result = shard_levels(key, dims, split, -0.22, 0.18) * result
    return jnp.clip(result, min=-bound, max=bound).astype(held_as)


def setup_inputs(seed: int = 0) -> dict:
    streams_of = jax.random.split(jax.random.key(seed), 10)
    return {
        "query_proj": normal_values(streams_of[0], (ROWS, SEQ, CH), 1.0, 6.0, ((0, 4), (1, 8))),
        "key_proj": normal_values(streams_of[1], (ROWS, SEQ, CH), 1.0, 6.0, ((0, 4), (1, 8))),
        "value_proj": normal_values(streams_of[2], (ROWS, SEQ, CH), 1.0, 6.0, ((0, 4), (1, 8))),
        "doc_offset": draw_doc_offset(jax.random.fold_in(streams_of[9], 71), 0),
        "short_taps": normal_values(streams_of[4], (3, TAPS, CH), 0.4, 2.5, (), jnp.float32),
        "rate_scale": jnp.clip(jnp.exp(jax.random.uniform(streams_of[5], (ORDER, CH), jnp.float32, math.log(0.1), math.log(120.0))), 0.1, 120.0),
        "residue": normal_values(streams_of[6], (ORDER, CH), 0.25, 2.5, (), jnp.float32),
        "skip_gain": jnp.clip(jax.random.uniform(streams_of[7], (CH,), jnp.float32, 0.5, 1.5), 0.5, 1.5),
        "out_grad": normal_values(streams_of[8], (ROWS, SEQ, CH), 1.0, 6.0, ((0, 4), (1, 8))),
    }


def delayed(values, shift_by):
    if shift_by == 0:
        return values
    head = jnp.zeros((shift_by,) + values.shape[1:], values.dtype)
    return jnp.concatenate([head, values[:-shift_by]], axis=0)

def advanced(values, shift_by):
    if shift_by == 0:
        return values
    tail = jnp.zeros((shift_by,) + values.shape[1:], values.dtype)
    return jnp.concatenate([values[shift_by:], tail], axis=0)

def one_row(query_row, key_row, value_row, grad_row, offsets, short_taps, rate_scale, residue, skip_gain):
    lam_log = -rate_scale / SEQ
    decay_step = jnp.exp(lam_log)
    norm_factor = jnp.sqrt(-jnp.expm1(2.0 * lam_log))
    mode_coef = residue * norm_factor
    tap_count = short_taps.shape[1]
    sources = [query_row.astype(jnp.float32), key_row.astype(jnp.float32), value_row.astype(jnp.float32)]
    filtered = []
    for branch_index in range(3):
        summed = jnp.zeros_like(sources[branch_index])
        for tap_index in range(tap_count):
            inside_doc = (offsets >= tap_index)[:, None]
            summed = summed + short_taps[branch_index, tap_index] * jnp.where(inside_doc, delayed(sources[branch_index], tap_index), 0.0)
        filtered.append(summed)
    query_short, key_short, value_short = filtered
    mixed = key_short * value_short
    grad_in = grad_row.astype(jnp.float32)
    z_grad = grad_in * query_short
    continues = (offsets > 0).astype(jnp.float32)

    def forward_step(carry, inputs):
        modal_state, res_accum = carry
        mixed_now, grad_now, cont_now = inputs
        modal_state = decay_step * cont_now * modal_state + mixed_now[None, :]
        res_accum = res_accum + grad_now[None, :] * modal_state
        return ((modal_state, res_accum), lax.optimization_barrier(jnp.sum(mode_coef * modal_state, axis=0)))
    zero_state = jnp.zeros(rate_scale.shape, jnp.float32)
    (_, res_accum), long_out = lax.scan(forward_step, (zero_state, zero_state), (mixed, z_grad, continues))
    z_full = long_out + skip_gain * mixed
    mixed_out = (query_short * z_full).astype(jnp.bfloat16)
    cont_next = jnp.concatenate([continues[1:], jnp.zeros((1,), jnp.float32)])

    def backward_step(carried, inputs):
        grad_now, cont_now = inputs
        carried = grad_now[None, :] + decay_step * cont_now * carried
        return (carried, lax.optimization_barrier(jnp.sum(mode_coef * carried, axis=0)))
    _, long_back = lax.scan(backward_step, zero_state, (z_grad, cont_next), reverse=True)
    mixed_grad = long_back + skip_gain * z_grad
    short_grads = [grad_in * z_full, mixed_grad * value_short, mixed_grad * key_short]
    input_grads = []
    tap_terms = []
    for branch_index in range(3):
        branch_grad = short_grads[branch_index]
        summed = jnp.zeros_like(branch_grad)
        per_tap = []
        for tap_index in range(tap_count):
            masked = jnp.where((offsets >= tap_index)[:, None], branch_grad, 0.0)
            summed = summed + short_taps[branch_index, tap_index] * advanced(masked, tap_index)
            per_tap.append(lax.optimization_barrier(jnp.sum(masked * delayed(sources[branch_index], tap_index), axis=0)))
        input_grads.append(summed.astype(jnp.bfloat16))
        tap_terms.append(jnp.stack(per_tap))
    skip_term = lax.optimization_barrier(jnp.sum(z_grad * mixed, axis=0))
    return (mixed_out, input_grads[0], input_grads[1], input_grads[2], jnp.stack(tap_terms), skip_term, norm_factor * res_accum)

def reference(query_proj, key_proj, value_proj, doc_offset, short_taps, rate_scale, residue, skip_gain, out_grad):

    def per_row(pieces):
        return one_row(pieces[0], pieces[1], pieces[2], pieces[3], pieces[4], short_taps, rate_scale, residue, skip_gain)
    results = lax.map(per_row, (query_proj, key_proj, value_proj, out_grad, doc_offset))
    scale = 1.0 / math.sqrt(ROWS * SEQ)
    taps_grad = lax.optimization_barrier(jnp.sum(results[4], axis=0)) * scale
    skip_grad = lax.optimization_barrier(jnp.sum(results[5], axis=0)) * scale
    residue_grad = lax.optimization_barrier(jnp.sum(results[6], axis=0)) * scale
    return (results[0], results[1], results[2], results[3], taps_grad, skip_grad, residue_grad)
```

```python
import functools
import math

import jax
import jax.numpy as jnp
from jax import lax
from jax.experimental import pallas as pl
from jax.experimental.pallas import tpu as pltpu
from jax.sharding import PartitionSpec as P

F32 = jnp.float32
BF16 = jnp.bfloat16
SUB = 8
LANES = 128
MESH = pl.DeviceIdType.MESH


def decay_powers(lam):
    powers = [jnp.ones_like(lam)]
    for _ in range(SUB - 1):
        powers.append(powers[-1] * lam)
    return powers


def cols_of(step):
    return pl.ds(pl.multiple_of(step * LANES, LANES), LANES)


def fill_extended(ext_ref, branch, rim_ref, source, cols):
    ext_ref[branch, 0:SUB, :] = rim_ref[branch, :, cols]
    ext_ref[branch, SUB:, :] = source


def local_kernel(
    taps,
    q_ref,
    k_ref,
    v_ref,
    og_ref,
    rim_ref,
    offs_ref,
    valid_ref,
    last_ref,
    pass_ref,
    short_ref,
    lamlog_ref,
    qs_ref,
    ks_ref,
    vs_ref,
    sig_ref,
    gam_ref,
    bsum_ref,
    badj_ref,
    ext_ref,
    xm_ref,
    zm_ref,
):
    tok, width = q_ref.shape

    def subtile(step, carry):
        cols = cols_of(step)
        offs = offs_ref[...]
        outs = []
        for branch, (ref, out) in enumerate(((q_ref, qs_ref), (k_ref, ks_ref), (v_ref, vs_ref))):
            source = ref[:, cols].astype(F32)
            fill_extended(ext_ref, branch, rim_ref, source, cols)
            total = short_ref[branch, 0:1, cols] * source
            for tap in range(1, taps):
                window = ext_ref[branch, SUB - tap : SUB - tap + tok, :]
                total = total + short_ref[branch, tap : tap + 1, cols] * jnp.where(
                    offs >= float(tap), window, 0.0
                )
            out[:, cols] = total
            outs.append(total)
        xm_ref[...] = outs[1] * outs[2] * last_ref[...]
        zm_ref[...] = og_ref[:, cols].astype(F32) * outs[0] * valid_ref[...]
        lam = jnp.exp(lamlog_ref[:, cols])
        powers = decay_powers(lam)
        span = powers[SUB - 1] * lam

        def sub_block(block, state):
            total, adjoint, weight = state
            base = block * SUB
            sigma = xm_ref[pl.ds(base + SUB - 1, 1), :] * powers[0]
            gamma = zm_ref[pl.ds(base, 1), :] * powers[0]
            for pos in range(1, SUB):
                sigma = sigma + powers[pos] * xm_ref[pl.ds(base + SUB - 1 - pos, 1), :]
                gamma = gamma + powers[pos] * zm_ref[pl.ds(base + pos, 1), :]
            sig_ref[block, :, cols] = sigma
            gam_ref[block, :, cols] = gamma
            factor = span * pass_ref[pl.ds(block, 1), :]
            return (sigma + factor * total, adjoint + weight * gamma, weight * factor)

        zero = jnp.zeros_like(lam)
        total, adjoint, _ = lax.fori_loop(
            0, tok // SUB, sub_block, (zero, zero, jnp.ones_like(lam)), unroll=4
        )
        bsum_ref[:, cols] = total
        badj_ref[:, cols] = adjoint
        return carry

    lax.fori_loop(0, width // LANES, subtile, 0)


def main_kernel(
    taps,
    q_ref,
    k_ref,
    v_ref,
    og_ref,
    rim_ref,
    qs_ref,
    ks_ref,
    vs_ref,
    sig_ref,
    gam_ref,
    enter_ref,
    adj_ref,
    offx_ref,
    offin_ref,
    valid_ref,
    last_ref,
    pass_ref,
    short_ref,
    lamlog_ref,
    coef_ref,
    norm_ref,
    skip_ref,
    mo_ref,
    qg_ref,
    kg_ref,
    vg_ref,
    head_ref,
    tail_ref,
    acc_ref,
    src_ref,
    g_ref,
    mo_scr,
    enters_scr,
    exits_scr,
    fwd_scr,
    bwd_scr,
    filt_scr,
):
    tok, width = q_ref.shape
    blocks = tok // SUB
    modes = lamlog_ref.shape[0]
    rows = lax.broadcasted_iota(jnp.int32, (SUB, LANES), 0).astype(F32)

    def subtile(step, carry):
        cols = cols_of(step)
        lamlog = lamlog_ref[:, cols]
        coef = coef_ref[:, cols]
        lam = jnp.exp(lamlog)
        powers = decay_powers(lam)
        span = powers[SUB - 1] * lam
        for lag in range(SUB):
            filt_scr[lag : lag + 1, :] = jnp.sum(coef * powers[lag], axis=0, keepdims=True)
        for mode in range(modes):
            log_row = lamlog[mode : mode + 1, :]
            coef_row = coef[mode : mode + 1, :]
            fwd_scr[mode] = coef_row * jnp.exp(log_row * (rows + 1.0))
            bwd_scr[mode] = coef_row * jnp.exp(log_row * (float(SUB) - rows))

        def sweep(index, state):
            forward, backward = state
            back = blocks - 1 - index
            enters_scr[index] = forward
            exits_scr[back] = backward
            forward = sig_ref[index, :, cols] + span * pass_ref[pl.ds(index, 1), :] * forward
            backward = gam_ref[back, :, cols] + span * pass_ref[pl.ds(back, 1), :] * backward
            return forward, backward

        lax.fori_loop(0, blocks, sweep, (enter_ref[:, cols], adj_ref[:, cols]), unroll=4)

        for branch, ref in enumerate((q_ref, k_ref, v_ref)):
            fill_extended(src_ref, branch, rim_ref, ref[:, cols].astype(F32), cols)
            g_ref[branch, 0:SUB, :] = jnp.zeros((SUB, LANES), F32)
            g_ref[branch, SUB + tok :, :] = jnp.zeros((SUB, LANES), F32)
        mo_scr[...] = og_ref[:, cols].astype(F32)
        skip = skip_ref[:, cols]

        def sub_block(block, state):
            lag_sums, res = state
            at = pl.ds(pl.multiple_of(block * SUB, SUB), SUB)
            query = qs_ref[at, cols]
            key = ks_ref[at, cols]
            value = vs_ref[at, cols]
            grad = mo_scr[at, :]
            mixed = key * value
            z_grad = grad * query
            offin = offin_ref[at, :]
            cross = jnp.zeros((SUB, LANES), F32)
            cross_back = jnp.zeros((SUB, LANES), F32)
            for mode in range(modes):
                cross = cross + fwd_scr[mode] * enters_scr[block, mode : mode + 1, :]
                cross_back = cross_back + bwd_scr[mode] * exits_scr[block, mode : mode + 1, :]
            first = filt_scr[0:1, :]
            forward = valid_ref[at, :] * cross + (first + skip) * mixed
            backward = last_ref[at, :] * cross_back + (first + skip) * z_grad
            new_sums = [lag_sums[0] + z_grad * mixed]
            for lag in range(1, SUB):
                inside = offin >= float(lag)
                tap = filt_scr[lag : lag + 1, :]
                shifted = jnp.where(inside, pltpu.roll(mixed, lag, 0), 0.0)
                forward = forward + tap * shifted
                new_sums.append(lag_sums[lag] + z_grad * shifted)
                backward = backward + tap * pltpu.roll(
                    jnp.where(inside, z_grad, 0.0), SUB - lag, 0
                )
            res = res + gam_ref[block, :, cols] * enters_scr[block]
            mo_scr[at, :] = query * forward
            put = pl.ds(pl.multiple_of(block * SUB + SUB, SUB), SUB)
            g_ref[0, put, :] = grad * forward
            g_ref[1, put, :] = backward * value
            g_ref[2, put, :] = backward * key
            return tuple(new_sums), res

        lag_sums, res = lax.fori_loop(
            0,
            blocks,
            sub_block,
            (
                tuple(jnp.zeros((SUB, LANES), F32) for _ in range(SUB)),
                jnp.zeros((modes, LANES), F32),
            ),
            unroll=2,
        )
        mo_ref[:, cols] = mo_scr[...].astype(BF16)
        res = res * lam
        sums = [jnp.sum(lag_sum, axis=0, keepdims=True) for lag_sum in lag_sums]
        for lag in range(SUB):
            res = res + powers[lag] * sums[lag]
        skip_row = 3 * taps
        res_row = acc_ref.shape[0] - modes
        acc_ref[skip_row:res_row, cols] = jnp.concatenate(
            [sums[0], jnp.zeros((res_row - skip_row - 1, LANES), F32)], axis=0
        )
        acc_ref[res_row:, cols] = norm_ref[:, cols] * res

        span_rows = tok + SUB
        for branch, out in enumerate((qg_ref, kg_ref, vg_ref)):
            source = src_ref[branch]
            spread = jnp.zeros((span_rows, LANES), F32)
            for tap in range(taps):
                moved = g_ref[branch, tap : tap + span_rows, :]
                if tap > 0:
                    moved = jnp.where(offx_ref[tap : tap + span_rows, :] >= float(tap), moved, 0.0)
                spread = spread + short_ref[branch, tap : tap + 1, cols] * moved
                row = branch * taps + tap
                acc_ref[row : row + 1, cols] = jnp.sum(source * moved, axis=0, keepdims=True)
            head_ref[branch, :, cols] = spread[0:SUB, :]
            out[:, cols] = spread[SUB:, :].astype(BF16)
            tail_ref[branch, :, cols] = spread[span_rows - 2 * SUB :, :]
        return carry

    lax.fori_loop(0, width // LANES, subtile, 0)


def hop_list(count):
    hops = [1]
    reach = 1
    while reach < count - 1:
        hops.append(reach)
        reach *= 2
    return hops


def state_kernel(
    tok,
    count,
    chunks,
    bsum_ref,
    badj_ref,
    lamlog_ref,
    mask_ref,
    enter_ref,
    adj_ref,
    fsend,
    frecv,
    bsend,
    brecv,
    fsem_s,
    fsem_r,
    bsem_s,
    bsem_r,
):
    hops = hop_list(count)
    me = lax.axis_index("ctx")
    barrier = pltpu.get_barrier_semaphore()
    partners = 0
    for hop in sorted(set(hops)):
        for sign in (1, -1):
            other = me + sign * hop
            there = jnp.logical_and(other >= 0, other < count)

            @pl.when(there)
            def _():
                pl.semaphore_signal(
                    barrier, inc=1, device_id={"ctx": other}, device_id_type=MESH
                )

            partners = partners + there.astype(jnp.int32)
    pl.semaphore_wait(barrier, partners)
    width = bsum_ref.shape[1] // chunks

    def copies(step, chunk):
        hop = hops[step]
        forward = pltpu.make_async_remote_copy(
            src_ref=fsend.at[step, chunk],
            dst_ref=frecv.at[step, chunk],
            send_sem=fsem_s.at[step, chunk],
            recv_sem=fsem_r.at[step, chunk],
            device_id={"ctx": me + hop},
            device_id_type=MESH,
        )
        backward = pltpu.make_async_remote_copy(
            src_ref=bsend.at[step, chunk],
            dst_ref=brecv.at[step, chunk],
            send_sem=bsem_s.at[step, chunk],
            recv_sem=bsem_r.at[step, chunk],
            device_id={"ctx": me - hop},
            device_id_type=MESH,
        )
        return forward, backward, me + hop < count, me - hop >= 0

    def start(step, chunk):
        forward, backward, upper, lower = copies(step, chunk)

        @pl.when(upper)
        def _():
            forward.start()

        @pl.when(lower)
        def _():
            backward.start()

    def mask_row(row):
        return jnp.concatenate([mask_ref[row : row + 1, :]] * (width // LANES), axis=1)

    steps = len(hops)
    for chunk in range(chunks):
        cols = slice(chunk * width, (chunk + 1) * width)
        fsend[0, chunk] = bsum_ref[:, cols]
        bsend[0, chunk] = badj_ref[:, cols] * mask_row(steps)
        start(0, chunk)
    for step in range(steps):
        for chunk in range(chunks):
            cols = slice(chunk * width, (chunk + 1) * width)
            forward, backward, upper, lower = copies(step, chunk)
            fmask = mask_row(step)
            if step > 0:
                decay = jnp.exp(float(tok * hops[step]) * lamlog_ref[:, cols])

            @pl.when(lower)
            def _():
                forward.wait_recv()
                if step == 0:
                    enter_ref[:, cols] = fmask * frecv[step, chunk]
                else:
                    enter_ref[:, cols] = (
                        enter_ref[:, cols] + decay * fmask * frecv[step, chunk]
                    )

            if step == 0:

                @pl.when(jnp.logical_not(lower))
                def _():
                    enter_ref[:, cols] = jnp.zeros((bsum_ref.shape[0], width), F32)

                @pl.when(jnp.logical_not(upper))
                def _():
                    adj_ref[:, cols] = jnp.zeros((bsum_ref.shape[0], width), F32)

            @pl.when(upper)
            def _():
                backward.wait_recv()
                if step == 0:
                    adj_ref[:, cols] = brecv[step, chunk]
                else:
                    adj_ref[:, cols] = adj_ref[:, cols] + decay * brecv[step, chunk]

            if step + 1 < steps:
                fsend[step + 1, chunk] = enter_ref[:, cols]
                bsend[step + 1, chunk] = adj_ref[:, cols] * mask_row(steps + step + 1)
                start(step + 1, chunk)
    for step in range(steps):
        for chunk in range(chunks):
            forward, backward, upper, lower = copies(step, chunk)

            @pl.when(upper)
            def _():
                forward.wait_send()

            @pl.when(lower)
            def _():
                backward.wait_send()


def reduce_kernel(
    dp_count,
    ctx_count,
    scale,
    acc_ref,
    out_ref,
    dp_recv,
    part,
    ctx_recv,
    full,
    s1,
    r1,
    s2,
    r2,
    s3,
    r3,
    s4,
    r4,
):
    dp = lax.axis_index("dp")
    ctx = lax.axis_index("ctx")
    channels = acc_ref.shape[1]
    wide = channels // dp_count
    narrow = wide // ctx_count
    barrier = pltpu.get_barrier_semaphore()
    for step in range(1, dp_count):
        pl.semaphore_signal(
            barrier, 1, device_id={"dp": (dp + step) % dp_count}, device_id_type=MESH
        )
    for step in range(1, ctx_count):
        pl.semaphore_signal(
            barrier, 1, device_id={"ctx": (ctx + step) % ctx_count}, device_id_type=MESH
        )
    pl.semaphore_wait(barrier, dp_count + ctx_count - 2)

    def wide_cols(index):
        return pl.ds(pl.multiple_of(index * wide, wide), wide)

    def narrow_cols(index):
        return pl.ds(pl.multiple_of(index * narrow, narrow), narrow)

    sent = []
    for step in range(1, dp_count):
        peer = (dp + step) % dp_count
        copy = pltpu.make_async_remote_copy(
            src_ref=acc_ref.at[:, wide_cols(peer)],
            dst_ref=dp_recv.at[step - 1],
            send_sem=s1.at[step - 1],
            recv_sem=r1.at[step - 1],
            device_id={"dp": peer},
            device_id_type=MESH,
        )
        copy.start()
        sent.append(copy)
    total = acc_ref[:, wide_cols(dp)]
    for step, copy in enumerate(sent):
        copy.wait_recv()
        total = total + dp_recv[step]
    part[...] = total
    ring = []
    for step in range(1, ctx_count):
        peer = (ctx + step) % ctx_count
        copy = pltpu.make_async_remote_copy(
            src_ref=part.at[:, narrow_cols(peer)],
            dst_ref=ctx_recv.at[step - 1],
            send_sem=s2.at[step - 1],
            recv_sem=r2.at[step - 1],
            device_id={"ctx": peer},
            device_id_type=MESH,
        )
        copy.start()
        ring.append(copy)
    total = part[:, narrow_cols(ctx)]
    for step, copy in enumerate(ring):
        copy.wait_recv()
        total = total + ctx_recv[step]
    mine = pl.ds(pl.multiple_of(dp * wide + ctx * narrow, narrow), narrow)
    full[:, mine] = total * scale
    sent += ring
    ring = []
    for step in range(1, ctx_count):
        peer = (ctx + step) % ctx_count
        copy = pltpu.make_async_remote_copy(
            src_ref=full.at[:, mine],
            dst_ref=full.at[:, mine],
            send_sem=s3.at[step - 1],
            recv_sem=r3.at[step - 1],
            device_id={"ctx": peer},
            device_id_type=MESH,
        )
        copy.start()
        ring.append(copy)
    for copy in ring:
        copy.wait_recv()
    sent += ring
    ring = []
    for step in range(1, dp_count):
        peer = (dp + step) % dp_count
        copy = pltpu.make_async_remote_copy(
            src_ref=full.at[:, wide_cols(dp)],
            dst_ref=full.at[:, wide_cols(dp)],
            send_sem=s4.at[step - 1],
            recv_sem=r4.at[step - 1],
            device_id={"dp": peer},
            device_id_type=MESH,
        )
        copy.start()
        ring.append(copy)
    for copy in ring:
        copy.wait_recv()
    out_ref[...] = full[...]
    for copy in sent + ring:
        copy.wait_send()


def reduce_all(acc, scale):
    dp_count = lax.axis_size("dp")
    ctx_count = lax.axis_size("ctx")
    rows, channels = acc.shape
    if channels % (dp_count * ctx_count * LANES) != 0:
        return lax.psum(acc, ("dp", "ctx")) * scale
    wide = channels // dp_count
    narrow = wide // ctx_count
    dma = pltpu.SemaphoreType.DMA
    return pl.pallas_call(
        functools.partial(reduce_kernel, dp_count, ctx_count, scale),
        out_shape=jax.ShapeDtypeStruct(acc.shape, F32),
        in_specs=[pl.BlockSpec(memory_space=pltpu.VMEM)],
        out_specs=pl.BlockSpec(memory_space=pltpu.VMEM),
        scratch_shapes=[
            pltpu.VMEM((dp_count - 1, rows, wide), F32),
            pltpu.VMEM((rows, wide), F32),
            pltpu.VMEM((ctx_count - 1, rows, narrow), F32),
            pltpu.VMEM((rows, channels), F32),
            dma((dp_count - 1,)),
            dma((dp_count - 1,)),
            dma((ctx_count - 1,)),
            dma((ctx_count - 1,)),
            dma((ctx_count - 1,)),
            dma((ctx_count - 1,)),
            dma((dp_count - 1,)),
            dma((dp_count - 1,)),
        ],
        compiler_params=pltpu.CompilerParams(
            collective_id=1, has_side_effects=True, vmem_limit_bytes=16 << 20
        ),
        name="reduce_grads",
    )(acc)


def exchange_states(tok, bsum, badj, lam_log, masks):
    count = lax.axis_size("ctx")
    steps = len(hop_list(count))
    chunks = 2
    modes, channels = bsum.shape
    dma = pltpu.SemaphoreType.DMA
    slot = pltpu.VMEM((steps, chunks, modes, channels // chunks), F32)
    return pl.pallas_call(
        functools.partial(state_kernel, tok, count, chunks),
        out_shape=[jax.ShapeDtypeStruct(bsum.shape, F32)] * 2,
        in_specs=[pl.BlockSpec(memory_space=pltpu.VMEM)] * 4,
        out_specs=[pl.BlockSpec(memory_space=pltpu.VMEM)] * 2,
        scratch_shapes=[slot] * 4 + [dma((steps, chunks))] * 4,
        compiler_params=pltpu.CompilerParams(
            collective_id=0, has_side_effects=True, vmem_limit_bytes=24 << 20
        ),
        name="exchange_states",
    )(bsum, badj, lam_log, masks)


def from_behind(block, distance):
    devices = range(lax.axis_size("ctx"))
    route = [(i - distance, i) for i in devices if i - distance in devices]
    return lax.ppermute(block, "ctx", route)


def shards(
    query_proj,
    key_proj,
    value_proj,
    doc_offset,
    short_taps,
    rate_scale,
    residue,
    skip_gain,
    out_grad,
):
    row_count, tok, channels = query_proj.shape
    ctx_count = lax.axis_size("ctx")
    seq_len = tok * ctx_count
    total_tokens = row_count * lax.axis_size("dp") * seq_len
    taps = short_taps.shape[1]
    modes = rate_scale.shape[0]
    rim = taps - 1
    blocks = tok // SUB
    query, key, value, grad = query_proj[0], key_proj[0], value_proj[0], out_grad[0]
    edge = jnp.stack([query[tok - rim :], key[tok - rim :], value[tok - rim :]], axis=0)
    edge = from_behind(edge, 1)
    edge = jnp.pad(edge.astype(F32), ((0, 0), (SUB - rim, 0), (0, 0)))

    lam_log = -rate_scale / seq_len
    norm = jnp.sqrt(-jnp.expm1(2.0 * lam_log))
    coef = residue * norm

    offs = doc_offset[0]
    index = jnp.arange(tok, dtype=jnp.int32) % SUB
    ends = offs.reshape(blocks, SUB)[:, SUB - 1]

    def wide(values):
        return jnp.broadcast_to(values.astype(F32)[:, None], (values.shape[0], LANES))

    offs_wide = wide(offs)
    offs_ext = jnp.pad(offs_wide, ((SUB, SUB), (0, 0)))
    offs_in = wide(jnp.minimum(offs, index))
    valid = wide(offs > index)
    last = wide(index >= SUB - 1 - jnp.repeat(ends, SUB))
    passes = wide(ends >= SUB)
    hops = hop_list(ctx_count)
    receive = [offs[0] >= 1] + [offs[0] >= tok * hop + 1 for hop in hops[1:]]
    send = [offs[0] >= 1] + [offs[tok - 1] >= tok * hop for hop in hops[1:]]
    masks = wide(jnp.stack(receive + send))

    width = 512 if channels % 512 == 0 else LANES
    grid = (channels // width,)

    def tile(*lead):
        zeros = (0,) * len(lead)
        return pl.BlockSpec(lead + (width,), lambda i: zeros + (i,))

    def whole(array):
        zeros = (0,) * array.ndim
        return pl.BlockSpec(array.shape, lambda i: zeros)

    def out(*dims, dtype=F32):
        return jax.ShapeDtypeStruct(dims + (channels,), dtype)

    token_tile = tile(tok)
    mode_tile = tile(modes)
    params = pltpu.CompilerParams(
        dimension_semantics=("arbitrary",), vmem_limit_bytes=48 << 20
    )
    qs, ks, vs, sig, gam, bsum, badj = pl.pallas_call(
        functools.partial(local_kernel, taps),
        grid=grid,
        out_shape=[out(tok)] * 3 + [out(blocks, modes)] * 2 + [out(modes)] * 2,
        in_specs=[token_tile] * 4
        + [tile(3, SUB)]
        + [whole(a) for a in (offs_wide, valid, last, passes)]
        + [tile(3, taps), mode_tile],
        out_specs=[token_tile] * 3 + [tile(blocks, modes)] * 2 + [mode_tile] * 2,
        scratch_shapes=[
            pltpu.VMEM((3, SUB + tok, LANES), F32),
            pltpu.VMEM((tok, LANES), F32),
            pltpu.VMEM((tok, LANES), F32),
        ],
        compiler_params=params,
        name="local_states",
    )(query, key, value, grad, edge, offs_wide, valid, last, passes, short_taps, lam_log)

    enter, adj = exchange_states(tok, bsum, badj, lam_log, masks)

    acc_rows = -(-(3 * taps + 1) // SUB) * SUB + modes
    skip_row = skip_gain[None, :]
    mixed_out, qg, kg, vg, heads, tails, acc = pl.pallas_call(
        functools.partial(main_kernel, taps),
        grid=grid,
        out_shape=[out(tok, dtype=BF16)] * 4 + [out(3, SUB), out(3, 2 * SUB), out(acc_rows)],
        in_specs=[token_tile] * 4
        + [tile(3, SUB)]
        + [token_tile] * 3
        + [tile(blocks, modes)] * 2
        + [mode_tile] * 2
        + [whole(a) for a in (offs_ext, offs_in, valid, last, passes)]
        + [tile(3, taps)]
        + [mode_tile] * 3
        + [tile(1)],
        out_specs=[token_tile] * 4 + [tile(3, SUB), tile(3, 2 * SUB), tile(acc_rows)],
        scratch_shapes=[
            pltpu.VMEM((3, SUB + tok, LANES), F32),
            pltpu.VMEM((3, tok + 2 * SUB, LANES), F32),
            pltpu.VMEM((tok, LANES), F32),
            pltpu.VMEM((blocks, modes, LANES), F32),
            pltpu.VMEM((blocks, modes, LANES), F32),
            pltpu.VMEM((modes, SUB, LANES), F32),
            pltpu.VMEM((modes, SUB, LANES), F32),
            pltpu.VMEM((SUB, LANES), F32),
        ],
        compiler_params=params,
        name="main_grads",
    )(
        query,
        key,
        value,
        grad,
        edge,
        qs,
        ks,
        vs,
        sig,
        gam,
        enter,
        adj,
        offs_ext,
        offs_in,
        valid,
        last,
        passes,
        short_taps,
        lam_log,
        coef,
        norm,
        skip_row,
    )
    incoming = from_behind(heads, -1)
    fixed = (tails + jnp.pad(incoming, ((0, 0), (SUB, 0), (0, 0)))).astype(BF16)
    grads = [
        lax.dynamic_update_slice(g, fixed[branch], (tok - 2 * SUB, 0))[None]
        for branch, g in enumerate((qg, kg, vg))
    ]
    sums = reduce_all(acc, 1.0 / math.sqrt(total_tokens))
    return (
        mixed_out[None],
        grads[0],
        grads[1],
        grads[2],
        sums[: 3 * taps].reshape(3, taps, channels),
        sums[3 * taps],
        sums[acc_rows - modes :],
    )


def solution(mesh):
    tokens = P("dp", "ctx", None)
    in_specs = (tokens, tokens, tokens, P("dp", "ctx"), P(), P(), P(), P(), tokens)
    out_specs = (tokens, tokens, tokens, tokens, P(), P(), P())
    return jax.shard_map(shards, mesh=mesh, in_specs=in_specs, out_specs=out_specs, check_vma=False)
```

```python
import functools
import math

import jax
import jax.numpy as jnp
from jax import lax
from jax.experimental import pallas as pl
from jax.experimental.pallas import tpu as pltpu
from jax.sharding import PartitionSpec as P

F32 = jnp.float32
BF16 = jnp.bfloat16
SUB = 8
LANES = 128
MESH = pl.DeviceIdType.MESH


def decay_powers(lam):
    powers = [jnp.ones_like(lam)]
    for _ in range(SUB - 1):
        powers.append(powers[-1] * lam)
    return powers


def fused_kernel(
    cfg,
    q_ref,
    k_ref,
    v_ref,
    og_ref,
    offx_ref,
    offin_ref,
    valid_ref,
    last_ref,
    pass_ref,
    dev_ref,
    short_ref,
    lamlog_ref,
    coef_ref,
    norm_ref,
    skip_ref,
    mo_ref,
    qg_ref,
    kg_ref,
    vg_ref,
    taps_out,
    skip_out,
    res_out,
    qs_scr,
    ks_scr,
    vs_scr,
    sig_scr,
    gam_scr,
    rim_recv,
    ends,
    pair_recv,
    chain_out,
    chain_recv,
    flag_recv,
    head_send,
    head_recv,
    tail_scr,
    acc,
    dp_recv,
    part,
    ctx_recv,
    full,
    ext_ref,
    g_ref,
    xm_ref,
    zm_ref,
    enters_scr,
    exits_scr,
    fwd_scr,
    bwd_scr,
    filt_scr,
    flag_s,
    flag_r,
    rim_s,
    rim_r,
    pair_s,
    pair_r,
    ea_s,
    ea_r,
    eb_s,
    eb_r,
    head_s,
    head_r,
    s1,
    r1,
    s2,
    r2,
    s3,
    r3,
):
    taps, width, dp_count, count, fused, scale = cfg
    tok, channels = q_ref.shape
    modes = lamlog_ref.shape[0]
    blocks = tok // SUB
    chunks = channels // width
    tiles = width // LANES
    pairs = count // 2
    first_main = max(chunks, 2 + 2 * (pairs - 1))
    me = lax.axis_index("ctx")
    dp = lax.axis_index("dp")
    odd = me % 2
    pair = me // 2
    place = odd * pair + (1 - odd) * (pairs - 1 - pair)
    other_place = pairs - 1 - place
    lead = 2 * odd - 1
    partner = me - lead
    sources = (q_ref, k_ref, v_ref)
    rows = lax.broadcasted_iota(jnp.int32, (SUB, LANES), 0).astype(F32)

    barrier = pltpu.get_barrier_semaphore()
    if fused:
        others = dp_count * count - 1
        lin = dp * count + me

        def peer_of(step):
            peer = (lin + step) % (dp_count * count)
            return {"dp": peer // count, "ctx": peer % count}

        def greet(step, carry):
            pl.semaphore_signal(barrier, 1, device_id=peer_of(step), device_id_type=MESH)
            return carry

        lax.fori_loop(1, others + 1, greet, 0)
        pl.semaphore_wait(barrier, others)
    else:
        friends = 0
        for hop in (1, -1, 2, -2):
            friend = me + hop
            there = jnp.logical_and(friend >= 0, friend < count)

            @pl.when(there)
            def _():
                pl.semaphore_signal(
                    barrier, 1, device_id={"ctx": friend}, device_id_type=MESH
                )

            friends = friends + there.astype(jnp.int32)
        pl.semaphore_wait(barrier, friends)

    def remote(source, target, send, recv, device):
        return pltpu.make_async_remote_copy(
            src_ref=source,
            dst_ref=target,
            send_sem=send,
            recv_sem=recv,
            device_id=device,
            device_id_type=MESH,
        )

    def chunk_cols(chunk):
        return pl.ds(pl.multiple_of(chunk * width, width), width)

    def tile_cols(chunk, step):
        return pl.ds(pl.multiple_of(chunk * width + step * LANES, LANES), LANES)

    def lane_cols(step):
        return pl.ds(pl.multiple_of(step * LANES, LANES), LANES)

    def rim_copy(chunk, branch):
        return remote(
            sources[branch].at[tok - 2 * SUB : tok, chunk_cols(chunk)],
            rim_recv.at[chunk, branch],
            rim_s.at[chunk, branch],
            rim_r.at[chunk, branch],
            {"ctx": me + 1},
        )

    def pair_copy(chunk):
        return remote(
            ends.at[1 - odd, chunk],
            pair_recv.at[chunk],
            pair_s.at[chunk],
            pair_r.at[chunk],
            {"ctx": partner},
        )

    def chain_copy(chunk):
        return remote(
            chain_out.at[chunk],
            chain_recv.at[odd, chunk],
            ea_s.at[chunk],
            ea_r.at[chunk],
            {"ctx": me + 2 * lead},
        )

    def cross_copy(chunk):
        return remote(
            chain_out.at[chunk],
            chain_recv.at[odd, chunk],
            eb_s.at[chunk],
            eb_r.at[chunk],
            {"ctx": me + lead},
        )

    def cross_arrival(chunk):
        return remote(
            chain_out.at[chunk],
            chain_recv.at[1 - odd, chunk],
            eb_s.at[chunk],
            eb_r.at[chunk],
            {"ctx": me - lead},
        )

    def head_copy(chunk):
        return remote(
            head_send.at[chunk],
            head_recv.at[chunk],
            head_s.at[chunk],
            head_r.at[chunk],
            {"ctx": me - 1},
        )

    flag_copy = remote(dev_ref, flag_recv, flag_s, flag_r, {"ctx": partner})
    flag_copy.start()

    @pl.when(me + 1 < count)
    def _():
        def send(chunk, carry):
            for branch in range(3):
                rim_copy(chunk, branch).start()
            return carry

        lax.fori_loop(0, chunks, send, 0)

    @pl.when(me == 0)
    def _():
        rim_recv[...] = jnp.zeros(rim_recv.shape, BF16)

    @pl.when(place == 0)
    def _():
        chain_recv[odd] = jnp.zeros(chain_recv.shape[1:], F32)

    @pl.when(other_place == 0)
    def _():
        chain_recv[1 - odd] = jnp.zeros(chain_recv.shape[1:], F32)

    def fill(branch, chunk, step, cols):
        edge = rim_recv[chunk, branch, :, lane_cols(step)].astype(F32)
        ext_ref[branch, 0:SUB, :] = edge[SUB:, :]
        source = sources[branch][:, cols].astype(F32)
        ext_ref[branch, SUB:, :] = source
        return source

    def local_tile(chunk, step):
        cols = tile_cols(chunk, step)
        offs = offx_ref[SUB : SUB + tok, :]
        outs = []
        for branch, out in enumerate((qs_scr, ks_scr, vs_scr)):
            source = fill(branch, chunk, step, cols)
            total = short_ref[branch, 0:1, cols] * source
            for tap in range(1, taps):
                window = ext_ref[branch, SUB - tap : SUB - tap + tok, :]
                total = total + short_ref[branch, tap : tap + 1, cols] * jnp.where(
                    offs >= float(tap), window, 0.0
                )
            out[:, cols] = total
            outs.append(total)
        xm_ref[...] = outs[1] * outs[2] * last_ref[...]
        zm_ref[...] = og_ref[:, cols].astype(F32) * outs[0] * valid_ref[...]
        lam = jnp.exp(lamlog_ref[:, cols])
        powers = decay_powers(lam)
        span = powers[SUB - 1] * lam

        def sub_block(block, state):
            total, adjoint, weight = state
            base = block * SUB
            sigma = xm_ref[pl.ds(base + SUB - 1, 1), :] * powers[0]
            gamma = zm_ref[pl.ds(base, 1), :] * powers[0]
            for pos in range(1, SUB):
                sigma = sigma + powers[pos] * xm_ref[pl.ds(base + SUB - 1 - pos, 1), :]
                gamma = gamma + powers[pos] * zm_ref[pl.ds(base + pos, 1), :]
            sig_scr[block, :, cols] = sigma
            gam_scr[block, :, cols] = gamma
            factor = span * pass_ref[pl.ds(block, 1), :]
            return (sigma + factor * total, adjoint + weight * gamma, weight * factor)

        zero = jnp.zeros_like(lam)
        total, adjoint, _ = lax.fori_loop(
            0, blocks, sub_block, (zero, zero, jnp.ones_like(lam)), unroll=4
        )
        ends[1, chunk, :, lane_cols(step)] = total
        ends[0, chunk, :, lane_cols(step)] = adjoint

    def chain_tile(chunk, step):
        at = lane_cols(step)
        decay = jnp.exp(float(tok) * lamlog_ref[:, tile_cols(chunk, step)])
        state = (
            pair_recv[chunk, :, at]
            + decay * flag_recv[0:1, :] * chain_recv[odd, chunk, :, at]
        )
        chain_recv[odd, chunk, :, at] = state
        chain_out[chunk, :, at] = ends[odd, chunk, :, at] + decay * dev_ref[0:1, :] * state

    def main_tile(chunk, step):
        cols = tile_cols(chunk, step)
        at_lanes = lane_cols(step)
        lamlog = lamlog_ref[:, cols]
        coef = coef_ref[:, cols]
        lam = jnp.exp(lamlog)
        powers = decay_powers(lam)
        span = powers[SUB - 1] * lam
        for lag in range(SUB):
            filt_scr[lag : lag + 1, :] = jnp.sum(coef * powers[lag], axis=0, keepdims=True)
        for mode in range(modes):
            log_row = lamlog[mode : mode + 1, :]
            coef_row = coef[mode : mode + 1, :]
            fwd_scr[mode] = coef_row * jnp.exp(log_row * (rows + 1.0))
            bwd_scr[mode] = coef_row * jnp.exp(log_row * (float(SUB) - rows))

        def sweep(index, state):
            forward, backward = state
            back = blocks - 1 - index
            enters_scr[index] = forward
            exits_scr[back] = backward
            forward = sig_scr[index, :, cols] + span * pass_ref[pl.ds(index, 1), :] * forward
            backward = gam_scr[back, :, cols] + span * pass_ref[pl.ds(back, 1), :] * backward
            return forward, backward

        lax.fori_loop(
            0,
            blocks,
            sweep,
            (chain_recv[1, chunk, :, at_lanes], chain_recv[0, chunk, :, at_lanes]),
            unroll=4,
        )

        for branch in range(3):
            fill(branch, chunk, step, cols)
            g_ref[branch, 0:SUB, :] = jnp.zeros((SUB, LANES), F32)
            g_ref[branch, SUB + tok :, :] = jnp.zeros((SUB, LANES), F32)
        xm_ref[...] = og_ref[:, cols].astype(F32)
        skip = skip_ref[:, cols]

        def sub_block(block, state):
            lag_sums, res = state
            at = pl.ds(pl.multiple_of(block * SUB, SUB), SUB)
            query = qs_scr[at, cols]
            key = ks_scr[at, cols]
            value = vs_scr[at, cols]
            grad = xm_ref[at, :]
            mixed = key * value
            z_grad = grad * query
            offin = offin_ref[at, :]
            cross = jnp.zeros((SUB, LANES), F32)
            cross_back = jnp.zeros((SUB, LANES), F32)
            for mode in range(modes):
                cross = cross + fwd_scr[mode] * enters_scr[block, mode : mode + 1, :]
                cross_back = cross_back + bwd_scr[mode] * exits_scr[block, mode : mode + 1, :]
            first = filt_scr[0:1, :]
            forward = valid_ref[at, :] * cross + (first + skip) * mixed
            backward = last_ref[at, :] * cross_back + (first + skip) * z_grad
            new_sums = [lag_sums[0] + z_grad * mixed]
            for lag in range(1, SUB):
                inside = offin >= float(lag)
                tap = filt_scr[lag : lag + 1, :]
                shifted = jnp.where(inside, pltpu.roll(mixed, lag, 0), 0.0)
                forward = forward + tap * shifted
                new_sums.append(lag_sums[lag] + z_grad * shifted)
                backward = backward + tap * pltpu.roll(
                    jnp.where(inside, z_grad, 0.0), SUB - lag, 0
                )
            res = res + gam_scr[block, :, cols] * enters_scr[block]
            xm_ref[at, :] = query * forward
            put = pl.ds(pl.multiple_of(block * SUB + SUB, SUB), SUB)
            g_ref[0, put, :] = grad * forward
            g_ref[1, put, :] = backward * value
            g_ref[2, put, :] = backward * key
            return tuple(new_sums), res

        lag_sums, res = lax.fori_loop(
            0,
            blocks,
            sub_block,
            (
                tuple(jnp.zeros((SUB, LANES), F32) for _ in range(SUB)),
                jnp.zeros((modes, LANES), F32),
            ),
            unroll=2,
        )
        mo_ref[:, cols] = xm_ref[...].astype(BF16)
        res = res * lam
        sums = [jnp.sum(lag_sum, axis=0, keepdims=True) for lag_sum in lag_sums]
        for lag in range(SUB):
            res = res + powers[lag] * sums[lag]
        skip_row = 3 * taps
        res_row = acc.shape[1] - modes
        acc[chunk, skip_row:res_row, at_lanes] = jnp.concatenate(
            [sums[0], jnp.zeros((res_row - skip_row - 1, LANES), F32)], axis=0
        )
        acc[chunk, res_row:, at_lanes] = norm_ref[:, cols] * res

        span_rows = tok + SUB
        for branch, out in enumerate((qg_ref, kg_ref, vg_ref)):
            source = ext_ref[branch]
            spread = jnp.zeros((span_rows, LANES), F32)
            for tap in range(taps):
                moved = g_ref[branch, tap : tap + span_rows, :]
                if tap > 0:
                    moved = jnp.where(offx_ref[tap : tap + span_rows, :] >= float(tap), moved, 0.0)
                spread = spread + short_ref[branch, tap : tap + 1, cols] * moved
                row = branch * taps + tap
                acc[chunk, row : row + 1, at_lanes] = jnp.sum(
                    source * moved, axis=0, keepdims=True
                )
            head_send[chunk, branch, :, at_lanes] = spread[0:SUB, :]
            out[:, cols] = spread[SUB:, :].astype(BF16)
            tail_scr[chunk, branch, :, at_lanes] = spread[span_rows - 2 * SUB :, :]

    def each_tile(work, chunk):
        def one(step, carry):
            work(chunk, step)
            return carry

        lax.fori_loop(0, tiles, one, 0)

    def dp_copy(chunk, step):
        peer = (dp + step) % dp_count
        return remote(
            acc.at[chunk, :, lane_cols(peer)],
            dp_recv.at[chunk, step - 1],
            s1.at[chunk, step - 1],
            r1.at[chunk, step - 1],
            {"dp": peer},
        )

    def ctx_copy(chunk):
        slot = (me - chunk + count) % count - 1
        return remote(
            part.at[chunk], ctx_recv.at[slot], s2.at[chunk], r2.at[slot], {"ctx": chunk}
        )

    def ctx_arrival(slot):
        return remote(
            part.at[0], ctx_recv.at[slot], s2.at[0], r2.at[slot], {"ctx": partner}
        )

    mine = tile_cols(me, dp) if fused else None

    def spread_copy(step):
        return remote(
            full.at[:, mine], full.at[:, mine], s3.at[step - 1], r3.at[step - 1], peer_of(step)
        )

    flag_copy.wait()

    def slot_body(slot, carry):
        @pl.when(slot < chunks)
        def _():
            @pl.when(me > 0)
            def _():
                for branch in range(3):
                    rim_copy(slot, branch).wait_recv()

            each_tile(local_tile, slot)
            pair_copy(slot).start()

        link = slot - 2 - 2 * place

        @pl.when(jnp.logical_and(link >= 0, link < chunks))
        def _():
            pair_copy(link).wait_recv()

            @pl.when(place > 0)
            def _():
                chain_copy(link).wait_recv()

            each_tile(chain_tile, link)

            @pl.when(place < pairs - 1)
            def _():
                chain_copy(link).start()
                cross_copy(link).start()

        now = slot - first_main

        @pl.when(jnp.logical_and(now >= 0, now < chunks))
        def _():
            @pl.when(other_place > 0)
            def _():
                cross_arrival(now).wait_recv()

            each_tile(main_tile, now)

            @pl.when(me > 0)
            def _():
                head_copy(now).start()

            if fused:
                for step in range(1, dp_count):
                    dp_copy(now, step).start()

        done = now - 1

        @pl.when(jnp.logical_and(done >= 0, done < chunks))
        def _():
            if fused:
                total = acc[done, :, lane_cols(dp)]
                for step in range(1, dp_count):
                    dp_copy(done, step).wait_recv()
                    total = total + dp_recv[done, step - 1]
                part[done] = total

                @pl.when(done != me)
                def _():
                    ctx_copy(done).start()

            @pl.when(me + 1 < count)
            def _():
                head_copy(done).wait_recv()
                for branch, out in enumerate((qg_ref, kg_ref, vg_ref)):
                    tail = tail_scr[done, branch]
                    tail = jnp.concatenate(
                        [tail[0:SUB, :], tail[SUB:, :] + head_recv[done, branch]], axis=0
                    )
                    out[tok - 2 * SUB : tok, chunk_cols(done)] = tail.astype(BF16)

        if fused:

            @pl.when(now - 2 == me)
            def _():
                total = part[me]
                for index in range(count - 1):
                    ctx_arrival(index).wait_recv()
                    total = total + ctx_recv[index]
                full[:, mine] = total * scale

                def send(step, inner):
                    spread_copy(step).start()
                    return inner

                lax.fori_loop(1, others + 1, send, 0)

        return carry

    lax.fori_loop(0, first_main + chunks + 2, slot_body, 0)

    if fused:

        def arrive(step, carry):
            spread_copy(step).wait_recv()
            return carry

        lax.fori_loop(1, others + 1, arrive, 0)

    def emit(chunk, carry):
        cols = chunk_cols(chunk)
        sums = full[:, cols] if fused else acc[chunk]
        for branch in range(3):
            taps_out[branch, :, cols] = sums[branch * taps : (branch + 1) * taps, :]
        skip_out[:, cols] = sums[3 * taps : 3 * taps + 1, :]
        res_out[:, cols] = sums[sums.shape[0] - modes :, :]
        return carry

    lax.fori_loop(0, chunks, emit, 0)

    def drain(chunk, carry):
        pair_copy(chunk).wait_send()

        @pl.when(me + 1 < count)
        def _():
            for branch in range(3):
                rim_copy(chunk, branch).wait_send()

        @pl.when(place < pairs - 1)
        def _():
            chain_copy(chunk).wait_send()
            cross_copy(chunk).wait_send()

        @pl.when(me > 0)
        def _():
            head_copy(chunk).wait_send()

        if fused:
            for step in range(1, dp_count):
                dp_copy(chunk, step).wait_send()

            @pl.when(chunk != me)
            def _():
                ctx_copy(chunk).wait_send()

        return carry

    lax.fori_loop(0, chunks, drain, 0)
    if fused:

        def sent(step, carry):
            spread_copy(step).wait_send()
            return carry

        lax.fori_loop(1, others + 1, sent, 0)


def shards(
    query_proj,
    key_proj,
    value_proj,
    doc_offset,
    short_taps,
    rate_scale,
    residue,
    skip_gain,
    out_grad,
):
    row_count, tok, channels = query_proj.shape
    count = lax.axis_size("ctx")
    dp_count = lax.axis_size("dp")
    seq_len = tok * count
    scale = 1.0 / math.sqrt(row_count * dp_count * seq_len)
    taps = short_taps.shape[1]
    modes = rate_scale.shape[0]
    blocks = tok // SUB
    fused = channels == dp_count * count * LANES
    width = dp_count * LANES if fused else 4 * LANES
    chunks = channels // width

    lam_log = -rate_scale / seq_len
    norm = jnp.sqrt(-jnp.expm1(2.0 * lam_log))
    coef = residue * norm

    offs = doc_offset[0]
    index = jnp.arange(tok, dtype=jnp.int32) % SUB
    ends = offs.reshape(blocks, SUB)[:, SUB - 1]

    def wide(values):
        return jnp.broadcast_to(values.astype(F32)[:, None], (values.shape[0], LANES))

    offs_ext = jnp.pad(wide(offs), ((SUB, SUB), (0, 0)))
    offs_in = wide(jnp.minimum(offs, index))
    valid = wide(offs > index)
    last = wide(index >= SUB - 1 - jnp.repeat(ends, SUB))
    passes = wide(ends >= SUB)
    whole_doc = wide(jnp.broadcast_to(offs[tok - 1] >= tok, (SUB,)))

    acc_rows = -(-(3 * taps + 1) // SUB) * SUB + modes
    dma = pltpu.SemaphoreType.DMA
    vmem = pl.BlockSpec(memory_space=pltpu.VMEM)
    dp_steps, ctx_steps = max(dp_count - 1, 1), max(count - 1, 1)
    all_steps = dp_count * count - 1 if fused else 1

    def scr(*dims, dtype=F32):
        return pltpu.VMEM(dims, dtype)

    outs = pl.pallas_call(
        functools.partial(fused_kernel, (taps, width, dp_count, count, fused, scale)),
        out_shape=[jax.ShapeDtypeStruct((tok, channels), BF16)] * 4
        + [
            jax.ShapeDtypeStruct((3, taps, channels), F32),
            jax.ShapeDtypeStruct((1, channels), F32),
            jax.ShapeDtypeStruct((modes, channels), F32),
        ],
        in_specs=[vmem] * 15,
        out_specs=[vmem] * 7,
        scratch_shapes=[scr(tok, channels)] * 3
        + [scr(blocks, modes, channels)] * 2
        + [
            scr(chunks, 3, 2 * SUB, width, dtype=BF16),
            scr(2, chunks, modes, width),
            scr(chunks, modes, width),
            scr(chunks, modes, width),
            scr(2, chunks, modes, width),
            scr(SUB, LANES),
            scr(chunks, 3, SUB, width),
            scr(chunks, 3, SUB, width),
            scr(chunks, 3, 2 * SUB, width),
            scr(chunks, acc_rows, width),
            scr(chunks, dp_steps, acc_rows, LANES),
            scr(chunks, acc_rows, LANES),
            scr(ctx_steps, acc_rows, LANES),
            scr(acc_rows, channels),
            scr(3, SUB + tok, LANES),
            scr(3, tok + 2 * SUB, LANES),
            scr(tok, LANES),
            scr(tok, LANES),
            scr(blocks, modes, LANES),
            scr(blocks, modes, LANES),
            scr(modes, SUB, LANES),
            scr(modes, SUB, LANES),
            scr(SUB, LANES),
            dma,
            dma,
        ]
        + [dma((chunks, 3))] * 2
        + [dma((chunks,))] * 8
        + [dma((chunks, dp_steps))] * 2
        + [dma((chunks,)), dma((ctx_steps,))]
        + [dma((all_steps,))] * 2,
        compiler_params=pltpu.CompilerParams(
            collective_id=0, has_side_effects=True, vmem_limit_bytes=56 << 20
        ),
        name="hyena_fused",
    )(
        query_proj[0],
        key_proj[0],
        value_proj[0],
        out_grad[0],
        offs_ext,
        offs_in,
        valid,
        last,
        passes,
        whole_doc,
        short_taps,
        lam_log,
        coef,
        norm,
        skip_gain[None, :],
    )
    sums = (outs[4], outs[5][0], outs[6])
    if not fused:
        sums = tuple(s * scale for s in lax.psum(sums, ("dp", "ctx")))
    return tuple(o[None] for o in outs[:4]) + sums


def solution(mesh):
    tokens = P("dp", "ctx", None)
    in_specs = (tokens, tokens, tokens, P("dp", "ctx"), P(), P(), P(), P(), tokens)
    out_specs = (tokens, tokens, tokens, tokens, P(), P(), P())
    return jax.shard_map(shards, mesh=mesh, in_specs=in_specs, out_specs=out_specs, check_vma=False)
```

```python
import functools
import math

import jax
import jax.numpy as jnp
from jax import lax
from jax.experimental import pallas as pl
from jax.experimental.pallas import tpu as pltpu
from jax.sharding import PartitionSpec as P

F32 = jnp.float32
BF16 = jnp.bfloat16
SUB = 8
LANES = 128
MESH = pl.DeviceIdType.MESH


def decay_powers(lam):
    powers = [jnp.ones_like(lam)]
    for _ in range(SUB - 1):
        powers.append(powers[-1] * lam)
    return powers


def fused_kernel(
    cfg,
    q_ref,
    k_ref,
    v_ref,
    og_ref,
    offx_ref,
    short_ref,
    lamlog_ref,
    coef_ref,
    norm_ref,
    skip_ref,
    mo_ref,
    qg_ref,
    kg_ref,
    vg_ref,
    taps_out,
    skip_out,
    res_out,
    qs_scr,
    ks_scr,
    vs_scr,
    sig_scr,
    gam_scr,
    offin_ref,
    valid_ref,
    last_ref,
    pass_ref,
    dev_ref,
    edge_scr,
    pack_scr,
    rim_scr,
    rim_send,
    rim_recv,
    ends,
    pair_recv,
    chain_out,
    chain_recv,
    flag_recv,
    head_send,
    head_recv,
    tail_scr,
    acc,
    dp_recv,
    part,
    ctx_recv,
    full,
    ext_ref,
    g_ref,
    xm_ref,
    zm_ref,
    enters_scr,
    exits_scr,
    fwd_scr,
    bwd_scr,
    filt_scr,
    flag_s,
    flag_r,
    rim_s,
    rim_r,
    pair_s,
    pair_r,
    ea_s,
    ea_r,
    eb_s,
    eb_r,
    head_s,
    head_r,
    s1,
    r1,
    s2,
    r2,
    s3,
    r3,
    s4,
    r4,
):
    taps, width, dp_count, count, fused, scale = cfg
    tok, channels = q_ref.shape
    modes = lamlog_ref.shape[0]
    blocks = tok // SUB
    chunks = channels // width
    tiles = width // LANES
    pairs = count // 2
    first_main = max(chunks, 3 + (5 * (pairs - 1)) // 3)
    me = lax.axis_index("ctx")
    dp = lax.axis_index("dp")
    odd = me % 2
    pair = me // 2
    place = odd * pair + (1 - odd) * (pairs - 1 - pair)
    other_place = pairs - 1 - place
    lead = 2 * odd - 1
    partner = me - lead
    sources = (q_ref, k_ref, v_ref)
    rows = lax.broadcasted_iota(jnp.int32, (SUB, LANES), 0).astype(F32)

    rim = taps - 1

    def build_masks(block, carry):
        at = pl.ds(pl.multiple_of(block * SUB, SUB), SUB)
        offs = offx_ref[pl.ds(pl.multiple_of(block * SUB + SUB, SUB), SUB), :]
        end = offx_ref[pl.ds(block * SUB + 2 * SUB - 1, 1), :]
        offin_ref[at, :] = jnp.minimum(offs, rows)
        valid_ref[at, :] = jnp.where(offs > rows, 1.0, 0.0)
        last_ref[at, :] = jnp.where(rows >= float(SUB - 1) - end, 1.0, 0.0)
        pass_ref[pl.ds(block, 1), :] = jnp.where(end >= float(SUB), 1.0, 0.0)
        return carry

    barrier = pltpu.get_barrier_semaphore()
    friends = 0
    if fused:
        for step in range(1, dp_count):
            pl.semaphore_signal(
                barrier, 1, device_id={"dp": (dp + step) % dp_count}, device_id_type=MESH
            )
        for step in range(1, count):
            pl.semaphore_signal(
                barrier, 1, device_id={"ctx": (me + step) % count}, device_id_type=MESH
            )
        friends = dp_count + count - 2
    else:
        for hop in (1, -1, 2, -2):
            friend = me + hop
            there = jnp.logical_and(friend >= 0, friend < count)

            @pl.when(there)
            def _():
                pl.semaphore_signal(
                    barrier, 1, device_id={"ctx": friend}, device_id_type=MESH
                )

            friends = friends + there.astype(jnp.int32)
    lax.fori_loop(0, blocks, build_masks, 0)
    dev_ref[...] = jnp.where(
        jnp.broadcast_to(offx_ref[SUB + tok - 1 : SUB + tok, :], (SUB, LANES)) >= float(tok),
        1.0,
        0.0,
    )

    def pack(chunk, carry):
        cols = pl.ds(pl.multiple_of(chunk * width, width), width)
        for branch, ref in enumerate(sources):
            edge_scr[...] = ref[tok - 2 * SUB : tok, cols].astype(F32)
            pack_scr[branch * rim : (branch + 1) * rim, :] = edge_scr[2 * SUB - rim :, :]
        rim_send[chunk] = pack_scr[...].astype(BF16)
        return carry

    pack_scr[...] = jnp.zeros(pack_scr.shape, F32)
    lax.fori_loop(0, chunks, pack, 0)
    pl.semaphore_wait(barrier, friends)

    def remote(source, target, send, recv, device):
        return pltpu.make_async_remote_copy(
            src_ref=source,
            dst_ref=target,
            send_sem=send,
            recv_sem=recv,
            device_id=device,
            device_id_type=MESH,
        )

    def chunk_cols(chunk):
        return pl.ds(pl.multiple_of(chunk * width, width), width)

    def tile_cols(chunk, step):
        return pl.ds(pl.multiple_of(chunk * width + step * LANES, LANES), LANES)

    def lane_cols(step):
        return pl.ds(pl.multiple_of(step * LANES, LANES), LANES)

    def rim_copy(chunk):
        return remote(
            rim_send.at[chunk],
            rim_recv.at[chunk],
            rim_s.at[chunk],
            rim_r.at[chunk],
            {"ctx": me + 1},
        )

    def pair_copy(chunk):
        return remote(
            ends.at[1 - odd, chunk],
            pair_recv.at[chunk],
            pair_s.at[chunk],
            pair_r.at[chunk],
            {"ctx": partner},
        )

    def chain_copy(chunk):
        return remote(
            chain_out.at[chunk],
            chain_recv.at[odd, chunk],
            ea_s.at[chunk],
            ea_r.at[chunk],
            {"ctx": me + 2 * lead},
        )

    def cross_copy(chunk):
        return remote(
            chain_out.at[chunk],
            chain_recv.at[odd, chunk],
            eb_s.at[chunk],
            eb_r.at[chunk],
            {"ctx": me + lead},
        )

    def cross_arrival(chunk):
        return remote(
            chain_out.at[chunk],
            chain_recv.at[1 - odd, chunk],
            eb_s.at[chunk],
            eb_r.at[chunk],
            {"ctx": me - lead},
        )

    def head_copy(chunk):
        return remote(
            head_send.at[chunk],
            head_recv.at[chunk],
            head_s.at[chunk],
            head_r.at[chunk],
            {"ctx": me - 1},
        )

    flag_copy = remote(dev_ref, flag_recv, flag_s, flag_r, {"ctx": partner})
    flag_copy.start()

    @pl.when(me + 1 < count)
    def _():
        def send(chunk, carry):
            rim_copy(chunk).start()
            return carry

        lax.fori_loop(0, chunks, send, 0)

    @pl.when(me == 0)
    def _():
        rim_recv[...] = jnp.zeros(rim_recv.shape, BF16)

    @pl.when(place == 0)
    def _():
        chain_recv[odd] = jnp.zeros(chain_recv.shape[1:], F32)

    @pl.when(other_place == 0)
    def _():
        chain_recv[1 - odd] = jnp.zeros(chain_recv.shape[1:], F32)

    def fill(branch, chunk, step, cols):
        if branch == 0:
            rim_scr[...] = rim_recv[chunk, :, lane_cols(step)].astype(F32)
        ext_ref[branch, 0:SUB, :] = jnp.zeros((SUB, LANES), F32)
        ext_ref[branch, SUB - rim : SUB, :] = rim_scr[branch * rim : (branch + 1) * rim, :]
        source = sources[branch][:, cols].astype(F32)
        ext_ref[branch, SUB:, :] = source
        return source

    def local_tile(chunk, step):
        cols = tile_cols(chunk, step)
        offs = offx_ref[SUB : SUB + tok, :]
        outs = []
        for branch, out in enumerate((qs_scr, ks_scr, vs_scr)):
            source = fill(branch, chunk, step, cols)
            total = short_ref[branch, 0:1, cols] * source
            for tap in range(1, taps):
                window = ext_ref[branch, SUB - tap : SUB - tap + tok, :]
                total = total + short_ref[branch, tap : tap + 1, cols] * jnp.where(
                    offs >= float(tap), window, 0.0
                )
            out[:, cols] = total
            outs.append(total)
        xm_ref[...] = outs[1] * outs[2] * last_ref[...]
        zm_ref[...] = og_ref[:, cols].astype(F32) * outs[0] * valid_ref[...]
        lam = jnp.exp(lamlog_ref[:, cols])
        powers = decay_powers(lam)
        span = powers[SUB - 1] * lam

        def sub_block(block, state):
            total, adjoint, weight = state
            base = block * SUB
            sigma = xm_ref[pl.ds(base + SUB - 1, 1), :] * powers[0]
            gamma = zm_ref[pl.ds(base, 1), :] * powers[0]
            for pos in range(1, SUB):
                sigma = sigma + powers[pos] * xm_ref[pl.ds(base + SUB - 1 - pos, 1), :]
                gamma = gamma + powers[pos] * zm_ref[pl.ds(base + pos, 1), :]
            sig_scr[block, :, cols] = sigma
            gam_scr[block, :, cols] = gamma
            factor = span * pass_ref[pl.ds(block, 1), :]
            return (sigma + factor * total, adjoint + weight * gamma, weight * factor)

        zero = jnp.zeros_like(lam)
        total, adjoint, _ = lax.fori_loop(
            0, blocks, sub_block, (zero, zero, jnp.ones_like(lam)), unroll=4
        )
        ends[1, chunk, :, lane_cols(step)] = total
        ends[0, chunk, :, lane_cols(step)] = adjoint

    def chain_tile(chunk, step):
        at = lane_cols(step)
        decay = jnp.exp(float(tok) * lamlog_ref[:, tile_cols(chunk, step)])
        state = (
            pair_recv[chunk, :, at]
            + decay * flag_recv[0:1, :] * chain_recv[odd, chunk, :, at]
        )
        chain_recv[odd, chunk, :, at] = state
        chain_out[chunk, :, at] = ends[odd, chunk, :, at] + decay * dev_ref[0:1, :] * state

    def main_tile(chunk, step):
        cols = tile_cols(chunk, step)
        at_lanes = lane_cols(step)
        lamlog = lamlog_ref[:, cols]
        coef = coef_ref[:, cols]
        lam = jnp.exp(lamlog)
        powers = decay_powers(lam)
        span = powers[SUB - 1] * lam
        for lag in range(SUB):
            filt_scr[lag : lag + 1, :] = jnp.sum(coef * powers[lag], axis=0, keepdims=True)
        for mode in range(modes):
            log_row = lamlog[mode : mode + 1, :]
            coef_row = coef[mode : mode + 1, :]
            fwd_scr[mode] = coef_row * jnp.exp(log_row * (rows + 1.0))
            bwd_scr[mode] = coef_row * jnp.exp(log_row * (float(SUB) - rows))

        def sweep(index, state):
            forward, backward = state
            back = blocks - 1 - index
            enters_scr[index] = forward
            exits_scr[back] = backward
            forward = sig_scr[index, :, cols] + span * pass_ref[pl.ds(index, 1), :] * forward
            backward = gam_scr[back, :, cols] + span * pass_ref[pl.ds(back, 1), :] * backward
            return forward, backward

        lax.fori_loop(
            0,
            blocks,
            sweep,
            (chain_recv[1, chunk, :, at_lanes], chain_recv[0, chunk, :, at_lanes]),
            unroll=4,
        )

        for branch in range(3):
            fill(branch, chunk, step, cols)
            g_ref[branch, 0:SUB, :] = jnp.zeros((SUB, LANES), F32)
            g_ref[branch, SUB + tok :, :] = jnp.zeros((SUB, LANES), F32)
        xm_ref[...] = og_ref[:, cols].astype(F32)
        skip = skip_ref[:, cols]

        def sub_block(block, state):
            lag_sums, res = state
            at = pl.ds(pl.multiple_of(block * SUB, SUB), SUB)
            query = qs_scr[at, cols]
            key = ks_scr[at, cols]
            value = vs_scr[at, cols]
            grad = xm_ref[at, :]
            mixed = key * value
            z_grad = grad * query
            offin = offin_ref[at, :]
            cross = jnp.zeros((SUB, LANES), F32)
            cross_back = jnp.zeros((SUB, LANES), F32)
            for mode in range(modes):
                cross = cross + fwd_scr[mode] * enters_scr[block, mode : mode + 1, :]
                cross_back = cross_back + bwd_scr[mode] * exits_scr[block, mode : mode + 1, :]
            first = filt_scr[0:1, :]
            forward = valid_ref[at, :] * cross + (first + skip) * mixed
            backward = last_ref[at, :] * cross_back + (first + skip) * z_grad
            new_sums = [lag_sums[0] + z_grad * mixed]
            for lag in range(1, SUB):
                inside = offin >= float(lag)
                tap = filt_scr[lag : lag + 1, :]
                shifted = jnp.where(inside, pltpu.roll(mixed, lag, 0), 0.0)
                forward = forward + tap * shifted
                new_sums.append(lag_sums[lag] + z_grad * shifted)
                backward = backward + tap * pltpu.roll(
                    jnp.where(inside, z_grad, 0.0), SUB - lag, 0
                )
            res = res + gam_scr[block, :, cols] * enters_scr[block]
            xm_ref[at, :] = query * forward
            put = pl.ds(pl.multiple_of(block * SUB + SUB, SUB), SUB)
            g_ref[0, put, :] = grad * forward
            g_ref[1, put, :] = backward * value
            g_ref[2, put, :] = backward * key
            return tuple(new_sums), res

        lag_sums, res = lax.fori_loop(
            0,
            blocks,
            sub_block,
            (
                tuple(jnp.zeros((SUB, LANES), F32) for _ in range(SUB)),
                jnp.zeros((modes, LANES), F32),
            ),
            unroll=2,
        )
        mo_ref[:, cols] = xm_ref[...].astype(BF16)
        res = res * lam
        sums = [jnp.sum(lag_sum, axis=0, keepdims=True) for lag_sum in lag_sums]
        for lag in range(SUB):
            res = res + powers[lag] * sums[lag]
        skip_row = 3 * taps
        res_row = acc.shape[1] - modes
        acc[chunk, skip_row:res_row, at_lanes] = jnp.concatenate(
            [sums[0], jnp.zeros((res_row - skip_row - 1, LANES), F32)], axis=0
        )
        acc[chunk, res_row:, at_lanes] = norm_ref[:, cols] * res

        span_rows = tok + SUB
        for branch, out in enumerate((qg_ref, kg_ref, vg_ref)):
            source = ext_ref[branch]
            spread = jnp.zeros((span_rows, LANES), F32)
            for tap in range(taps):
                moved = g_ref[branch, tap : tap + span_rows, :]
                if tap > 0:
                    moved = jnp.where(offx_ref[tap : tap + span_rows, :] >= float(tap), moved, 0.0)
                spread = spread + short_ref[branch, tap : tap + 1, cols] * moved
                row = branch * taps + tap
                acc[chunk, row : row + 1, at_lanes] = jnp.sum(
                    source * moved, axis=0, keepdims=True
                )
            head_send[chunk, branch, :, at_lanes] = spread[0:SUB, :]
            out[:, cols] = spread[SUB:, :].astype(BF16)
            tail_scr[chunk, branch, :, at_lanes] = spread[span_rows - 2 * SUB :, :]

    def each_tile(work, chunk):
        def one(step, carry):
            work(chunk, step)
            return carry

        lax.fori_loop(0, tiles, one, 0)

    def dp_copy(chunk, step):
        peer = (dp + step) % dp_count
        return remote(
            acc.at[chunk, :, lane_cols(peer)],
            dp_recv.at[chunk, step - 1],
            s1.at[chunk, step - 1],
            r1.at[chunk, step - 1],
            {"dp": peer},
        )

    def owner_of(chunk):
        return (chunk + count // 2) % count

    my_chunk = (me + count - count // 2) % count

    def ctx_copy(chunk):
        owner = owner_of(chunk)
        slot = (me - owner + count) % count - 1
        return remote(
            part.at[chunk], ctx_recv.at[slot], s2.at[chunk], r2.at[slot], {"ctx": owner}
        )

    def ctx_arrival(slot):
        return remote(
            part.at[0], ctx_recv.at[slot], s2.at[0], r2.at[slot], {"ctx": partner}
        )

    def gather_copy(chunk, step):
        place_cols = tile_cols(chunk, dp)
        return remote(
            full.at[:, place_cols],
            full.at[:, place_cols],
            s3.at[step - 1],
            r3.at[chunk],
            {"ctx": (me + step) % count},
        )

    def forward_copy(chunk, step):
        place_cols = tile_cols(chunk, dp)
        return remote(
            full.at[:, place_cols],
            full.at[:, place_cols],
            s4.at[chunk, step - 1],
            r4.at[chunk, step - 1],
            {"dp": (dp + step) % dp_count},
        )

    def forward_arrival(chunk, step):
        place_cols = tile_cols(chunk, (dp + dp_count - step) % dp_count)
        return remote(
            full.at[:, place_cols],
            full.at[:, place_cols],
            s4.at[chunk, step - 1],
            r4.at[chunk, step - 1],
            {"dp": (dp + step) % dp_count},
        )

    def sum_parts(done):
        total = acc[done, :, lane_cols(dp)]
        for step in range(1, dp_count):
            dp_copy(done, step).wait_recv()
            total = total + dp_recv[done, step - 1]
        part[done] = total

        @pl.when(owner_of(done) != me)
        def _():
            ctx_copy(done).start()

    flag_copy.wait()

    def slot_body(slot, carry):
        @pl.when(slot < chunks)
        def _():
            @pl.when(me > 0)
            def _():
                rim_copy(slot).wait_recv()

            each_tile(local_tile, slot)
            pair_copy(slot).start()

        link = slot - 3 - (5 * place) // 3

        @pl.when(jnp.logical_and(link >= 0, link < chunks))
        def _():
            pair_copy(link).wait_recv()

            @pl.when(place > 0)
            def _():
                chain_copy(link).wait_recv()

            each_tile(chain_tile, link)

            @pl.when(place < pairs - 1)
            def _():
                chain_copy(link).start()
                cross_copy(link).start()

        now = slot - first_main

        @pl.when(jnp.logical_and(now >= 0, now < chunks))
        def _():
            @pl.when(other_place > 0)
            def _():
                cross_arrival(now).wait_recv()

            def one(step, inner):
                if fused:

                    @pl.when(jnp.logical_and(step == tiles // 2, now > 0))
                    def _():
                        sum_parts(now - 1)

                main_tile(now, step)
                return inner

            lax.fori_loop(0, tiles, one, 0)

            @pl.when(me > 0)
            def _():
                head_copy(now).start()

            if fused:
                for step in range(1, dp_count):
                    dp_copy(now, step).start()

        done = now - 1

        @pl.when(jnp.logical_and(done >= 0, done < chunks))
        def _():
            if fused:

                @pl.when(done == chunks - 1)
                def _():
                    sum_parts(chunks - 1)

            @pl.when(me + 1 < count)
            def _():
                head_copy(done).wait_recv()
                for branch, out in enumerate((qg_ref, kg_ref, vg_ref)):
                    tail = tail_scr[done, branch]
                    tail = jnp.concatenate(
                        [tail[0:SUB, :], tail[SUB:, :] + head_recv[done, branch]], axis=0
                    )
                    out[tok - 2 * SUB : tok, chunk_cols(done)] = tail.astype(BF16)

        if fused:

            @pl.when(done == my_chunk)
            def _():
                total = part[my_chunk]
                for index in range(count - 1):
                    ctx_arrival(index).wait_recv()
                    total = total + ctx_recv[index]
                full[:, tile_cols(my_chunk, dp)] = total * scale
                for step in range(1, count):
                    gather_copy(my_chunk, step).start()

            ready = now - 2

            @pl.when(jnp.logical_and(ready >= 0, ready < chunks))
            def _():
                @pl.when(ready != my_chunk)
                def _():
                    gather_copy(ready, 1).wait_recv()

                for step in range(1, dp_count):
                    forward_copy(ready, step).start()

        return carry

    lax.fori_loop(0, first_main + chunks + 2, slot_body, 0)

    if fused:

        def arrive(chunk, carry):
            for step in range(1, dp_count):
                forward_arrival(chunk, step).wait_recv()
            return carry

        lax.fori_loop(0, chunks, arrive, 0)

    def emit(chunk, carry):
        cols = chunk_cols(chunk)
        sums = full[:, cols] if fused else acc[chunk]
        for branch in range(3):
            taps_out[branch, :, cols] = sums[branch * taps : (branch + 1) * taps, :]
        skip_out[:, cols] = sums[3 * taps : 3 * taps + 1, :]
        res_out[:, cols] = sums[sums.shape[0] - modes :, :]
        return carry

    lax.fori_loop(0, chunks, emit, 0)

    def drain(chunk, carry):
        pair_copy(chunk).wait_send()

        @pl.when(me + 1 < count)
        def _():
            rim_copy(chunk).wait_send()

        @pl.when(place < pairs - 1)
        def _():
            chain_copy(chunk).wait_send()
            cross_copy(chunk).wait_send()

        @pl.when(me > 0)
        def _():
            head_copy(chunk).wait_send()

        if fused:
            for step in range(1, dp_count):
                dp_copy(chunk, step).wait_send()

                forward_copy(chunk, step).wait_send()

            @pl.when(owner_of(chunk) != me)
            def _():
                ctx_copy(chunk).wait_send()

        return carry

    lax.fori_loop(0, chunks, drain, 0)
    if fused:
        for step in range(1, count):
            gather_copy(my_chunk, step).wait_send()


def settle_kernel(*refs):
    half = len(refs) // 2
    for source, target in zip(refs[:half], refs[half:]):
        target[...] = source[...]


def settle(arrays):
    channels = arrays[0].shape[-1]
    width = channels // 4

    def spec(array):
        zeros = (0,) * (array.ndim - 1)
        return pl.BlockSpec(array.shape[:-1] + (width,), lambda i: zeros + (i,))

    return pl.pallas_call(
        settle_kernel,
        grid=(4,),
        out_shape=[jax.ShapeDtypeStruct(a.shape, a.dtype) for a in arrays],
        in_specs=[spec(a) for a in arrays],
        out_specs=[spec(a) for a in arrays],
        compiler_params=pltpu.CompilerParams(
            dimension_semantics=("arbitrary",), vmem_limit_bytes=24 << 20
        ),
        name="settle_outputs",
    )(*arrays)


def shards(
    query_proj,
    key_proj,
    value_proj,
    doc_offset,
    short_taps,
    rate_scale,
    residue,
    skip_gain,
    out_grad,
):
    row_count, tok, channels = query_proj.shape
    count = lax.axis_size("ctx")
    dp_count = lax.axis_size("dp")
    seq_len = tok * count
    scale = 1.0 / math.sqrt(row_count * dp_count * seq_len)
    taps = short_taps.shape[1]
    modes = rate_scale.shape[0]
    blocks = tok // SUB
    fused = channels == dp_count * count * LANES
    width = dp_count * LANES if fused else 4 * LANES
    chunks = channels // width

    lam_log = -rate_scale / seq_len
    norm = jnp.sqrt(-jnp.expm1(2.0 * lam_log))
    coef = residue * norm

    offs = jnp.pad(doc_offset[0], (SUB, SUB)).astype(F32)
    offs_ext = jnp.broadcast_to(offs[:, None], (tok + 2 * SUB, LANES))

    acc_rows = -(-(3 * taps + 1) // SUB) * SUB + modes
    dma = pltpu.SemaphoreType.DMA
    vmem = pl.BlockSpec(memory_space=pltpu.VMEM)
    dp_steps, ctx_steps = max(dp_count - 1, 1), max(count - 1, 1)
    rim_rows = -(-3 * (taps - 1) // (2 * SUB)) * 2 * SUB

    def scr(*dims, dtype=F32):
        return pltpu.VMEM(dims, dtype)

    outs = pl.pallas_call(
        functools.partial(fused_kernel, (taps, width, dp_count, count, fused, scale)),
        out_shape=[jax.ShapeDtypeStruct((tok, channels), BF16)] * 4
        + [
            jax.ShapeDtypeStruct((3, taps, channels), F32),
            jax.ShapeDtypeStruct((1, channels), F32),
            jax.ShapeDtypeStruct((modes, channels), F32),
        ],
        in_specs=[vmem] * 10,
        out_specs=[vmem] * 7,
        scratch_shapes=[scr(tok, channels)] * 3
        + [scr(blocks, modes, channels)] * 2
        + [
            scr(tok, LANES),
            scr(tok, LANES),
            scr(tok, LANES),
            scr(blocks, LANES),
            scr(SUB, LANES),
            scr(2 * SUB, width),
            scr(rim_rows, width),
            scr(rim_rows, LANES),
            scr(chunks, rim_rows, width, dtype=BF16),
            scr(chunks, rim_rows, width, dtype=BF16),
            scr(2, chunks, modes, width),
            scr(chunks, modes, width),
            scr(chunks, modes, width),
            scr(2, chunks, modes, width),
            scr(SUB, LANES),
            scr(chunks, 3, SUB, width),
            scr(chunks, 3, SUB, width),
            scr(chunks, 3, 2 * SUB, width),
            scr(chunks, acc_rows, width),
            scr(chunks, dp_steps, acc_rows, LANES),
            scr(chunks, acc_rows, LANES),
            scr(ctx_steps, acc_rows, LANES),
            scr(acc_rows, channels),
            scr(3, SUB + tok, LANES),
            scr(3, tok + 2 * SUB, LANES),
            scr(tok, LANES),
            scr(tok, LANES),
            scr(blocks, modes, LANES),
            scr(blocks, modes, LANES),
            scr(modes, SUB, LANES),
            scr(modes, SUB, LANES),
            scr(SUB, LANES),
            dma,
            dma,
        ]
        + [dma((chunks,))] * 10
        + [dma((chunks, dp_steps))] * 2
        + [dma((chunks,)), dma((ctx_steps,))]
        + [dma((ctx_steps,)), dma((chunks,))]
        + [dma((chunks, dp_steps))] * 2,
        compiler_params=pltpu.CompilerParams(
            collective_id=0, has_side_effects=True, vmem_limit_bytes=56 << 20
        ),
        name="hyena_fused",
    )(
        query_proj[0],
        key_proj[0],
        value_proj[0],
        out_grad[0],
        offs_ext,
        short_taps,
        lam_log,
        coef,
        norm,
        skip_gain[None, :],
    )
    outs = settle(outs)
    sums = (outs[4], outs[5][0], outs[6])
    if not fused:
        sums = tuple(s * scale for s in lax.psum(sums, ("dp", "ctx")))
    return tuple(o[None] for o in outs[:4]) + sums


def solution(mesh):
    tokens = P("dp", "ctx", None)
    in_specs = (tokens, tokens, tokens, P("dp", "ctx"), P(), P(), P(), P(), tokens)
    out_specs = (tokens, tokens, tokens, tokens, P(), P(), P())
    return jax.shard_map(shards, mesh=mesh, in_specs=in_specs, out_specs=out_specs, check_vma=False)
```

```python
import functools
import math

import jax
import jax.numpy as jnp
from jax import lax
from jax.experimental import pallas as pl
from jax.experimental.pallas import tpu as pltpu
from jax.sharding import PartitionSpec as P

F32 = jnp.float32
BF16 = jnp.bfloat16
SUB = 8
LANES = 128
MESH = pl.DeviceIdType.MESH


def decay_powers(lam):
    powers = [jnp.ones_like(lam)]
    for _ in range(SUB - 1):
        powers.append(powers[-1] * lam)
    return powers


def fused_kernel(
    cfg,
    q_ref,
    k_ref,
    v_ref,
    og_ref,
    offx_ref,
    short_ref,
    lamlog_ref,
    coef_ref,
    norm_ref,
    skip_ref,
    mo_ref,
    qg_ref,
    kg_ref,
    vg_ref,
    taps_out,
    skip_out,
    res_out,
    qs_scr,
    ks_scr,
    vs_scr,
    sig_scr,
    gam_scr,
    offin_ref,
    valid_ref,
    last_ref,
    pass_ref,
    dev_ref,
    mask_scr,
    edge_scr,
    pack_scr,
    rim_scr,
    rim_send,
    rim_recv,
    ends,
    pair_recv,
    chain_out,
    chain_recv,
    flag_recv,
    head_send,
    head_recv,
    tail_scr,
    acc,
    dp_recv,
    part,
    ctx_recv,
    full,
    ext_ref,
    g_ref,
    xm_ref,
    zm_ref,
    enters_scr,
    exits_scr,
    fwd_scr,
    bwd_scr,
    filt_scr,
    flag_s,
    flag_r,
    rim_s,
    rim_r,
    pair_s,
    pair_r,
    ea_s,
    ea_r,
    eb_s,
    eb_r,
    head_s,
    head_r,
    s1,
    r1,
    s2,
    r2,
    s3,
    r3,
    s4,
    r4,
):
    taps, width, dp_count, count, fused, scale = cfg
    tok, channels = q_ref.shape
    modes = lamlog_ref.shape[0]
    blocks = tok // SUB
    chunks = channels // width
    tiles = width // LANES
    pairs = count // 2
    first_main = max(chunks, 3 + (5 * (pairs - 1)) // 3)
    me = lax.axis_index("ctx")
    dp = lax.axis_index("dp")
    odd = me % 2
    pair = me // 2
    place = odd * pair + (1 - odd) * (pairs - 1 - pair)
    other_place = pairs - 1 - place
    lead = 2 * odd - 1
    partner = me - lead
    sources = (q_ref, k_ref, v_ref)
    rows = lax.broadcasted_iota(jnp.int32, (SUB, LANES), 0).astype(F32)

    rim = taps - 1

    def build_masks(block, carry):
        at = pl.ds(pl.multiple_of(block * SUB, SUB), SUB)
        offs = offx_ref[pl.ds(pl.multiple_of(block * SUB + SUB, SUB), SUB), :]
        end = offx_ref[pl.ds(block * SUB + 2 * SUB - 1, 1), :]
        offin_ref[at, :] = jnp.minimum(offs, rows)
        valid_ref[at, :] = jnp.where(offs > rows, 1.0, 0.0)
        last_ref[at, :] = jnp.where(rows >= float(SUB - 1) - end, 1.0, 0.0)
        pass_ref[pl.ds(block, 1), :] = jnp.where(end >= float(SUB), 1.0, 0.0)
        return carry

    barrier = pltpu.get_barrier_semaphore()
    friends = 0
    if fused:
        for step in range(1, dp_count):
            pl.semaphore_signal(
                barrier, 1, device_id={"dp": (dp + step) % dp_count}, device_id_type=MESH
            )
        for step in range(1, count):
            pl.semaphore_signal(
                barrier, 1, device_id={"ctx": (me + step) % count}, device_id_type=MESH
            )
        friends = dp_count + count - 2
    else:
        for hop in (1, -1, 2, -2):
            friend = me + hop
            there = jnp.logical_and(friend >= 0, friend < count)

            @pl.when(there)
            def _():
                pl.semaphore_signal(
                    barrier, 1, device_id={"ctx": friend}, device_id_type=MESH
                )

            friends = friends + there.astype(jnp.int32)
    lax.fori_loop(0, blocks, build_masks, 0)
    for tap in range(1, taps):
        mask_scr[tap - 1] = jnp.where(
            offx_ref[tap : tap + tok + SUB, :] >= float(tap), 1.0, 0.0
        )
    dev_ref[...] = jnp.where(
        jnp.broadcast_to(offx_ref[SUB + tok - 1 : SUB + tok, :], (SUB, LANES)) >= float(tok),
        1.0,
        0.0,
    )

    def pack(chunk, carry):
        cols = pl.ds(pl.multiple_of(chunk * width, width), width)
        for branch, ref in enumerate(sources):
            edge_scr[...] = ref[tok - 2 * SUB : tok, cols].astype(F32)
            pack_scr[branch * rim : (branch + 1) * rim, :] = edge_scr[2 * SUB - rim :, :]
        rim_send[chunk] = pack_scr[...].astype(BF16)
        return carry

    pack_scr[...] = jnp.zeros(pack_scr.shape, F32)
    lax.fori_loop(0, chunks, pack, 0)
    pl.semaphore_wait(barrier, friends)

    def remote(source, target, send, recv, device):
        return pltpu.make_async_remote_copy(
            src_ref=source,
            dst_ref=target,
            send_sem=send,
            recv_sem=recv,
            device_id=device,
            device_id_type=MESH,
        )

    def chunk_cols(chunk):
        return pl.ds(pl.multiple_of(chunk * width, width), width)

    def tile_cols(chunk, step):
        return pl.ds(pl.multiple_of(chunk * width + step * LANES, LANES), LANES)

    def lane_cols(step):
        return pl.ds(pl.multiple_of(step * LANES, LANES), LANES)

    def rim_copy(chunk):
        return remote(
            rim_send.at[chunk],
            rim_recv.at[chunk],
            rim_s.at[chunk],
            rim_r.at[chunk],
            {"ctx": me + 1},
        )

    def pair_copy(chunk):
        return remote(
            ends.at[1 - odd, chunk],
            pair_recv.at[chunk],
            pair_s.at[chunk],
            pair_r.at[chunk],
            {"ctx": partner},
        )

    def chain_copy(chunk):
        return remote(
            chain_out.at[chunk],
            chain_recv.at[odd, chunk],
            ea_s.at[chunk],
            ea_r.at[chunk],
            {"ctx": me + 2 * lead},
        )

    def cross_copy(chunk):
        return remote(
            chain_out.at[chunk],
            chain_recv.at[odd, chunk],
            eb_s.at[chunk],
            eb_r.at[chunk],
            {"ctx": me + lead},
        )

    def cross_arrival(chunk):
        return remote(
            chain_out.at[chunk],
            chain_recv.at[1 - odd, chunk],
            eb_s.at[chunk],
            eb_r.at[chunk],
            {"ctx": me - lead},
        )

    def head_copy(chunk):
        return remote(
            head_send.at[chunk],
            head_recv.at[chunk],
            head_s.at[chunk],
            head_r.at[chunk],
            {"ctx": me - 1},
        )

    flag_copy = remote(dev_ref, flag_recv, flag_s, flag_r, {"ctx": partner})
    flag_copy.start()

    @pl.when(me + 1 < count)
    def _():
        def send(chunk, carry):
            rim_copy(chunk).start()
            return carry

        lax.fori_loop(0, chunks, send, 0)

    @pl.when(me == 0)
    def _():
        rim_recv[...] = jnp.zeros(rim_recv.shape, BF16)

    @pl.when(place == 0)
    def _():
        chain_recv[odd] = jnp.zeros(chain_recv.shape[1:], F32)

    @pl.when(other_place == 0)
    def _():
        chain_recv[1 - odd] = jnp.zeros(chain_recv.shape[1:], F32)

    def fill(branch, chunk, step, cols):
        if branch == 0:
            rim_scr[...] = rim_recv[chunk, :, lane_cols(step)].astype(F32)
        ext_ref[branch, 0:SUB, :] = jnp.zeros((SUB, LANES), F32)
        ext_ref[branch, SUB - rim : SUB, :] = rim_scr[branch * rim : (branch + 1) * rim, :]
        source = sources[branch][:, cols].astype(F32)
        ext_ref[branch, SUB:, :] = source
        return source

    def local_tile(chunk, step):
        cols = tile_cols(chunk, step)
        offs = offx_ref[SUB : SUB + tok, :]
        outs = []
        for branch, out in enumerate((qs_scr, ks_scr, vs_scr)):
            source = fill(branch, chunk, step, cols)
            total = short_ref[branch, 0:1, cols] * source
            for tap in range(1, taps):
                window = ext_ref[branch, SUB - tap : SUB - tap + tok, :]
                total = total + short_ref[branch, tap : tap + 1, cols] * jnp.where(
                    offs >= float(tap), window, 0.0
                )
            out[:, cols] = total
            outs.append(total)
        xm_ref[...] = outs[1] * outs[2] * last_ref[...]
        zm_ref[...] = og_ref[:, cols].astype(F32) * outs[0] * valid_ref[...]
        lam = jnp.exp(lamlog_ref[:, cols])
        powers = decay_powers(lam)
        span = powers[SUB - 1] * lam

        def sub_block(block, state):
            total, adjoint, weight = state
            base = block * SUB
            sigma = xm_ref[pl.ds(base + SUB - 1, 1), :] * powers[0]
            gamma = zm_ref[pl.ds(base, 1), :] * powers[0]
            for pos in range(1, SUB):
                sigma = sigma + powers[pos] * xm_ref[pl.ds(base + SUB - 1 - pos, 1), :]
                gamma = gamma + powers[pos] * zm_ref[pl.ds(base + pos, 1), :]
            sig_scr[block, :, cols] = sigma
            gam_scr[block, :, cols] = gamma
            factor = span * pass_ref[pl.ds(block, 1), :]
            return (sigma + factor * total, adjoint + weight * gamma, weight * factor)

        zero = jnp.zeros_like(lam)
        total, adjoint, _ = lax.fori_loop(
            0, blocks, sub_block, (zero, zero, jnp.ones_like(lam)), unroll=4
        )
        ends[1, chunk, :, lane_cols(step)] = total
        ends[0, chunk, :, lane_cols(step)] = adjoint

    def chain_tile(chunk, step):
        at = lane_cols(step)
        decay = jnp.exp(float(tok) * lamlog_ref[:, tile_cols(chunk, step)])
        state = (
            pair_recv[chunk, :, at]
            + decay * flag_recv[0:1, :] * chain_recv[odd, chunk, :, at]
        )
        chain_recv[odd, chunk, :, at] = state
        chain_out[chunk, :, at] = ends[odd, chunk, :, at] + decay * dev_ref[0:1, :] * state

    def main_tile(chunk, step):
        cols = tile_cols(chunk, step)
        at_lanes = lane_cols(step)
        lamlog = lamlog_ref[:, cols]
        coef = coef_ref[:, cols]
        lam = jnp.exp(lamlog)
        powers = decay_powers(lam)
        span = powers[SUB - 1] * lam
        for lag in range(SUB):
            filt_scr[lag : lag + 1, :] = jnp.sum(coef * powers[lag], axis=0, keepdims=True)
        for mode in range(modes):
            log_row = lamlog[mode : mode + 1, :]
            coef_row = coef[mode : mode + 1, :]
            fwd_scr[mode] = coef_row * jnp.exp(log_row * (rows + 1.0))
            bwd_scr[mode] = coef_row * jnp.exp(log_row * (float(SUB) - rows))

        def sweep(index, state):
            forward, backward = state
            back = blocks - 1 - index
            enters_scr[index] = forward
            exits_scr[back] = backward
            forward = sig_scr[index, :, cols] + span * pass_ref[pl.ds(index, 1), :] * forward
            backward = gam_scr[back, :, cols] + span * pass_ref[pl.ds(back, 1), :] * backward
            return forward, backward

        lax.fori_loop(
            0,
            blocks,
            sweep,
            (chain_recv[1, chunk, :, at_lanes], chain_recv[0, chunk, :, at_lanes]),
            unroll=4,
        )

        for branch in range(3):
            fill(branch, chunk, step, cols)
            g_ref[branch, 0:SUB, :] = jnp.zeros((SUB, LANES), F32)
            g_ref[branch, SUB + tok :, :] = jnp.zeros((SUB, LANES), F32)
        xm_ref[...] = og_ref[:, cols].astype(F32)
        skip = skip_ref[:, cols]

        def sub_block(block, state):
            lag_sums, res = state
            at = pl.ds(pl.multiple_of(block * SUB, SUB), SUB)
            query = qs_scr[at, cols]
            key = ks_scr[at, cols]
            value = vs_scr[at, cols]
            grad = xm_ref[at, :]
            mixed = key * value
            z_grad = grad * query
            offin = offin_ref[at, :]
            cross = jnp.zeros((SUB, LANES), F32)
            cross_back = jnp.zeros((SUB, LANES), F32)
            for mode in range(modes):
                cross = cross + fwd_scr[mode] * enters_scr[block, mode : mode + 1, :]
                cross_back = cross_back + bwd_scr[mode] * exits_scr[block, mode : mode + 1, :]
            first = filt_scr[0:1, :]
            forward = valid_ref[at, :] * cross + (first + skip) * mixed
            backward = last_ref[at, :] * cross_back + (first + skip) * z_grad
            new_sums = [lag_sums[0] + z_grad * mixed]
            for lag in range(1, SUB):
                inside = offin >= float(lag)
                tap = filt_scr[lag : lag + 1, :]
                shifted = jnp.where(inside, pltpu.roll(mixed, lag, 0), 0.0)
                forward = forward + tap * shifted
                new_sums.append(lag_sums[lag] + z_grad * shifted)
                backward = backward + tap * pltpu.roll(
                    jnp.where(inside, z_grad, 0.0), SUB - lag, 0
                )
            res = res + gam_scr[block, :, cols] * enters_scr[block]
            xm_ref[at, :] = query * forward
            put = pl.ds(pl.multiple_of(block * SUB + SUB, SUB), SUB)
            g_ref[0, put, :] = grad * forward
            g_ref[1, put, :] = backward * value
            g_ref[2, put, :] = backward * key
            return tuple(new_sums), res

        lag_sums, res = lax.fori_loop(
            0,
            blocks,
            sub_block,
            (
                tuple(jnp.zeros((SUB, LANES), F32) for _ in range(SUB)),
                jnp.zeros((modes, LANES), F32),
            ),
            unroll=4,
        )
        mo_ref[:, cols] = xm_ref[...].astype(BF16)
        res = res * lam
        sums = [jnp.sum(lag_sum, axis=0, keepdims=True) for lag_sum in lag_sums]
        for lag in range(SUB):
            res = res + powers[lag] * sums[lag]
        skip_row = 3 * taps
        res_row = acc.shape[1] - modes
        acc[chunk, skip_row:res_row, at_lanes] = jnp.concatenate(
            [sums[0], jnp.zeros((res_row - skip_row - 1, LANES), F32)], axis=0
        )
        acc[chunk, res_row:, at_lanes] = norm_ref[:, cols] * res

        span_rows = tok + SUB
        for branch, out in enumerate((qg_ref, kg_ref, vg_ref)):
            source = ext_ref[branch]
            spread = jnp.zeros((span_rows, LANES), F32)
            for tap in range(taps):
                moved = g_ref[branch, tap : tap + span_rows, :]
                if tap > 0:
                    moved = moved * mask_scr[tap - 1]
                spread = spread + short_ref[branch, tap : tap + 1, cols] * moved
                row = branch * taps + tap
                acc[chunk, row : row + 1, at_lanes] = jnp.sum(
                    source * moved, axis=0, keepdims=True
                )
            head_send[chunk, branch, :, at_lanes] = spread[0:SUB, :]
            out[:, cols] = spread[SUB:, :].astype(BF16)
            tail_scr[chunk, branch, :, at_lanes] = spread[span_rows - 2 * SUB :, :]

    def each_tile(work, chunk):
        def one(step, carry):
            work(chunk, step)
            return carry

        lax.fori_loop(0, tiles, one, 0)

    def dp_copy(chunk, step):
        peer = (dp + step) % dp_count
        return remote(
            acc.at[chunk, :, lane_cols(peer)],
            dp_recv.at[chunk, step - 1],
            s1.at[chunk, step - 1],
            r1.at[chunk, step - 1],
            {"dp": peer},
        )

    def owner_of(chunk):
        return (chunk + count // 2) % count

    my_chunk = (me + count - count // 2) % count

    def ctx_copy(chunk):
        owner = owner_of(chunk)
        slot = (me - owner + count) % count - 1
        return remote(
            part.at[chunk], ctx_recv.at[slot], s2.at[chunk], r2.at[slot], {"ctx": owner}
        )

    def ctx_arrival(slot):
        return remote(
            part.at[0], ctx_recv.at[slot], s2.at[0], r2.at[slot], {"ctx": partner}
        )

    def gather_copy(chunk, step):
        place_cols = tile_cols(chunk, dp)
        return remote(
            full.at[:, place_cols],
            full.at[:, place_cols],
            s3.at[step - 1],
            r3.at[chunk],
            {"ctx": (me + step) % count},
        )

    def forward_copy(chunk, step):
        place_cols = tile_cols(chunk, dp)
        return remote(
            full.at[:, place_cols],
            full.at[:, place_cols],
            s4.at[chunk, step - 1],
            r4.at[chunk, step - 1],
            {"dp": (dp + step) % dp_count},
        )

    def forward_arrival(chunk, step):
        place_cols = tile_cols(chunk, (dp + dp_count - step) % dp_count)
        return remote(
            full.at[:, place_cols],
            full.at[:, place_cols],
            s4.at[chunk, step - 1],
            r4.at[chunk, step - 1],
            {"dp": (dp + step) % dp_count},
        )

    def sum_parts(done):
        total = acc[done, :, lane_cols(dp)]
        for step in range(1, dp_count):
            dp_copy(done, step).wait_recv()
            total = total + dp_recv[done, step - 1]
        part[done] = total

        @pl.when(owner_of(done) != me)
        def _():
            ctx_copy(done).start()

    flag_copy.wait()

    def slot_body(slot, carry):
        @pl.when(slot < chunks)
        def _():
            @pl.when(me > 0)
            def _():
                rim_copy(slot).wait_recv()

            each_tile(local_tile, slot)
            pair_copy(slot).start()

        link = slot - 3 - (5 * place) // 3

        @pl.when(jnp.logical_and(link >= 0, link < chunks))
        def _():
            pair_copy(link).wait_recv()

            @pl.when(place > 0)
            def _():
                chain_copy(link).wait_recv()

            each_tile(chain_tile, link)

            @pl.when(place < pairs - 1)
            def _():
                chain_copy(link).start()
                cross_copy(link).start()

        now = slot - first_main

        @pl.when(jnp.logical_and(now >= 0, now < chunks))
        def _():
            @pl.when(other_place > 0)
            def _():
                cross_arrival(now).wait_recv()

            def one(step, inner):
                if fused:

                    @pl.when(jnp.logical_and(step == tiles // 2, now > 0))
                    def _():
                        sum_parts(now - 1)

                main_tile(now, step)
                return inner

            lax.fori_loop(0, tiles, one, 0)

            @pl.when(me > 0)
            def _():
                head_copy(now).start()

            if fused:
                for step in range(1, dp_count):
                    dp_copy(now, step).start()

        done = now - 1

        @pl.when(jnp.logical_and(done >= 0, done < chunks))
        def _():
            if fused:

                @pl.when(done == chunks - 1)
                def _():
                    sum_parts(chunks - 1)

            @pl.when(me + 1 < count)
            def _():
                head_copy(done).wait_recv()
                for branch, out in enumerate((qg_ref, kg_ref, vg_ref)):
                    tail = tail_scr[done, branch]
                    tail = jnp.concatenate(
                        [tail[0:SUB, :], tail[SUB:, :] + head_recv[done, branch]], axis=0
                    )
                    out[tok - 2 * SUB : tok, chunk_cols(done)] = tail.astype(BF16)

        if fused:

            @pl.when(done == my_chunk)
            def _():
                total = part[my_chunk]
                for index in range(count - 1):
                    ctx_arrival(index).wait_recv()
                    total = total + ctx_recv[index]
                full[:, tile_cols(my_chunk, dp)] = total * scale
                for step in range(1, count):
                    gather_copy(my_chunk, step).start()

            ready = now - 2

            @pl.when(jnp.logical_and(ready >= 0, ready < chunks))
            def _():
                @pl.when(ready != my_chunk)
                def _():
                    gather_copy(ready, 1).wait_recv()

                for step in range(1, dp_count):
                    forward_copy(ready, step).start()

        return carry

    lax.fori_loop(0, first_main + chunks + 2, slot_body, 0)

    if fused:

        def arrive(chunk, carry):
            for step in range(1, dp_count):
                forward_arrival(chunk, step).wait_recv()
            return carry

        lax.fori_loop(0, chunks, arrive, 0)

    def emit(chunk, carry):
        cols = chunk_cols(chunk)
        sums = full[:, cols] if fused else acc[chunk]
        for branch in range(3):
            taps_out[branch, :, cols] = sums[branch * taps : (branch + 1) * taps, :]
        skip_out[:, cols] = sums[3 * taps : 3 * taps + 1, :]
        res_out[:, cols] = sums[sums.shape[0] - modes :, :]
        return carry

    lax.fori_loop(0, chunks, emit, 0)

    def drain(chunk, carry):
        pair_copy(chunk).wait_send()

        @pl.when(me + 1 < count)
        def _():
            rim_copy(chunk).wait_send()

        @pl.when(place < pairs - 1)
        def _():
            chain_copy(chunk).wait_send()
            cross_copy(chunk).wait_send()

        @pl.when(me > 0)
        def _():
            head_copy(chunk).wait_send()

        if fused:
            for step in range(1, dp_count):
                dp_copy(chunk, step).wait_send()

                forward_copy(chunk, step).wait_send()

            @pl.when(owner_of(chunk) != me)
            def _():
                ctx_copy(chunk).wait_send()

        return carry

    lax.fori_loop(0, chunks, drain, 0)
    if fused:
        for step in range(1, count):
            gather_copy(my_chunk, step).wait_send()


def settle_kernel(*refs):
    half = len(refs) // 2
    for source, target in zip(refs[:half], refs[half:]):
        target[...] = source[...]


def settle(arrays):
    channels = arrays[0].shape[-1]
    width = channels // 4

    def spec(array):
        zeros = (0,) * (array.ndim - 1)
        return pl.BlockSpec(array.shape[:-1] + (width,), lambda i: zeros + (i,))

    return pl.pallas_call(
        settle_kernel,
        grid=(4,),
        out_shape=[jax.ShapeDtypeStruct(a.shape, a.dtype) for a in arrays],
        in_specs=[spec(a) for a in arrays],
        out_specs=[spec(a) for a in arrays],
        compiler_params=pltpu.CompilerParams(
            dimension_semantics=("arbitrary",), vmem_limit_bytes=56 << 20
        ),
        name="settle_outputs",
    )(*arrays)


def shards(
    query_proj,
    key_proj,
    value_proj,
    doc_offset,
    short_taps,
    rate_scale,
    residue,
    skip_gain,
    out_grad,
):
    row_count, tok, channels = query_proj.shape
    count = lax.axis_size("ctx")
    dp_count = lax.axis_size("dp")
    seq_len = tok * count
    scale = 1.0 / math.sqrt(row_count * dp_count * seq_len)
    taps = short_taps.shape[1]
    modes = rate_scale.shape[0]
    blocks = tok // SUB
    fused = channels == dp_count * count * LANES
    width = dp_count * LANES if fused else 4 * LANES
    chunks = channels // width

    lam_log = -rate_scale / seq_len
    norm = jnp.sqrt(-jnp.expm1(2.0 * lam_log))
    coef = residue * norm

    offs = jnp.pad(doc_offset[0], (SUB, SUB)).astype(F32)
    offs_ext = jnp.broadcast_to(offs[:, None], (tok + 2 * SUB, LANES))

    acc_rows = -(-(3 * taps + 1) // SUB) * SUB + modes
    dma = pltpu.SemaphoreType.DMA
    vmem = pl.BlockSpec(memory_space=pltpu.VMEM)
    dp_steps, ctx_steps = max(dp_count - 1, 1), max(count - 1, 1)
    rim_rows = -(-3 * (taps - 1) // (2 * SUB)) * 2 * SUB

    def scr(*dims, dtype=F32):
        return pltpu.VMEM(dims, dtype)

    outs = pl.pallas_call(
        functools.partial(fused_kernel, (taps, width, dp_count, count, fused, scale)),
        out_shape=[jax.ShapeDtypeStruct((tok, channels), BF16)] * 4
        + [
            jax.ShapeDtypeStruct((3, taps, channels), F32),
            jax.ShapeDtypeStruct((1, channels), F32),
            jax.ShapeDtypeStruct((modes, channels), F32),
        ],
        in_specs=[vmem] * 10,
        out_specs=[vmem] * 7,
        scratch_shapes=[scr(tok, channels)] * 3
        + [scr(blocks, modes, channels)] * 2
        + [
            scr(tok, LANES),
            scr(tok, LANES),
            scr(tok, LANES),
            scr(blocks, LANES),
            scr(SUB, LANES),
            scr(taps - 1, tok + SUB, LANES),
            scr(2 * SUB, width),
            scr(rim_rows, width),
            scr(rim_rows, LANES),
            scr(chunks, rim_rows, width, dtype=BF16),
            scr(chunks, rim_rows, width, dtype=BF16),
            scr(2, chunks, modes, width),
            scr(chunks, modes, width),
            scr(chunks, modes, width),
            scr(2, chunks, modes, width),
            scr(SUB, LANES),
            scr(chunks, 3, SUB, width),
            scr(chunks, 3, SUB, width),
            scr(chunks, 3, 2 * SUB, width),
            scr(chunks, acc_rows, width),
            scr(chunks, dp_steps, acc_rows, LANES),
            scr(chunks, acc_rows, LANES),
            scr(ctx_steps, acc_rows, LANES),
            scr(acc_rows, channels),
            scr(3, SUB + tok, LANES),
            scr(3, tok + 2 * SUB, LANES),
            scr(tok, LANES),
            scr(tok, LANES),
            scr(blocks, modes, LANES),
            scr(blocks, modes, LANES),
            scr(modes, SUB, LANES),
            scr(modes, SUB, LANES),
            scr(SUB, LANES),
            dma,
            dma,
        ]
        + [dma((chunks,))] * 10
        + [dma((chunks, dp_steps))] * 2
        + [dma((chunks,)), dma((ctx_steps,))]
        + [dma((ctx_steps,)), dma((chunks,))]
        + [dma((chunks, dp_steps))] * 2,
        compiler_params=pltpu.CompilerParams(
            collective_id=0, has_side_effects=True, vmem_limit_bytes=56 << 20
        ),
        name="hyena_fused",
    )(
        query_proj[0],
        key_proj[0],
        value_proj[0],
        out_grad[0],
        offs_ext,
        short_taps,
        lam_log,
        coef,
        norm,
        skip_gain[None, :],
    )
    outs = settle(outs)
    sums = (outs[4], outs[5][0], outs[6])
    if not fused:
        sums = tuple(s * scale for s in lax.psum(sums, ("dp", "ctx")))
    return tuple(o[None] for o in outs[:4]) + sums


def solution(mesh):
    tokens = P("dp", "ctx", None)
    in_specs = (tokens, tokens, tokens, P("dp", "ctx"), P(), P(), P(), P(), tokens)
    out_specs = (tokens, tokens, tokens, tokens, P(), P(), P())
    return jax.shard_map(shards, mesh=mesh, in_specs=in_specs, out_specs=out_specs, check_vma=False)
```

```python
import functools
import math

import jax
import jax.numpy as jnp
from jax import lax
from jax.experimental import pallas as pl
from jax.experimental.pallas import tpu as pltpu
from jax.sharding import PartitionSpec as P

F32 = jnp.float32
BF16 = jnp.bfloat16
SUB = 8
LANES = 128
MESH = pl.DeviceIdType.MESH


def decay_powers(lam):
    powers = [jnp.ones_like(lam)]
    for _ in range(SUB - 1):
        powers.append(powers[-1] * lam)
    return powers


def fused_kernel(
    cfg,
    q_ref,
    k_ref,
    v_ref,
    og_ref,
    offx_ref,
    short_ref,
    lamlog_ref,
    coef_ref,
    norm_ref,
    skip_ref,
    mo_ref,
    qg_ref,
    kg_ref,
    vg_ref,
    taps_out,
    skip_out,
    res_out,
    qs_scr,
    ks_scr,
    vs_scr,
    sig_scr,
    gam_scr,
    offin_ref,
    valid_ref,
    last_ref,
    pass_ref,
    dev_ref,
    mask_scr,
    edge_scr,
    pack_scr,
    rim_scr,
    rim_send,
    rim_recv,
    ends,
    pair_recv,
    chain_out,
    chain_recv,
    flag_recv,
    head_send,
    head_recv,
    tail_scr,
    acc,
    dp_recv,
    part,
    ctx_recv,
    full,
    ext_ref,
    g_ref,
    xm_ref,
    zm_ref,
    enters_scr,
    exits_scr,
    fwd_scr,
    bwd_scr,
    filt_scr,
    flag_s,
    flag_r,
    rim_s,
    rim_r,
    pair_s,
    pair_r,
    ea_s,
    ea_r,
    eb_s,
    eb_r,
    head_s,
    head_r,
    s1,
    r1,
    s2,
    r2,
    s3,
    r3,
    s4,
    r4,
):
    taps, width, dp_count, count, fused, scale = cfg
    tok, channels = q_ref.shape
    modes = lamlog_ref.shape[0]
    blocks = tok // SUB
    chunks = channels // width
    tiles = width // LANES
    pairs = count // 2
    first_main = max(chunks, 3 + (5 * (pairs - 1)) // 3)
    me = lax.axis_index("ctx")
    dp = lax.axis_index("dp")
    odd = me % 2
    pair = me // 2
    place = odd * pair + (1 - odd) * (pairs - 1 - pair)
    other_place = pairs - 1 - place
    lead = 2 * odd - 1
    partner = me - lead
    sources = (q_ref, k_ref, v_ref)
    rows = lax.broadcasted_iota(jnp.int32, (SUB, LANES), 0).astype(F32)

    rim = taps - 1

    def build_masks(block, carry):
        at = pl.ds(pl.multiple_of(block * SUB, SUB), SUB)
        offs = offx_ref[pl.ds(pl.multiple_of(block * SUB + SUB, SUB), SUB), :]
        end = offx_ref[pl.ds(block * SUB + 2 * SUB - 1, 1), :]
        offin_ref[at, :] = jnp.minimum(offs, rows)
        valid_ref[at, :] = jnp.where(offs > rows, 1.0, 0.0)
        last_ref[at, :] = jnp.where(rows >= float(SUB - 1) - end, 1.0, 0.0)
        pass_ref[pl.ds(block, 1), :] = jnp.where(end >= float(SUB), 1.0, 0.0)
        return carry

    barrier = pltpu.get_barrier_semaphore()
    friends = 0
    if fused:
        for step in range(1, dp_count):
            pl.semaphore_signal(
                barrier, 1, device_id={"dp": (dp + step) % dp_count}, device_id_type=MESH
            )
        for step in range(1, count):
            pl.semaphore_signal(
                barrier, 1, device_id={"ctx": (me + step) % count}, device_id_type=MESH
            )
        friends = dp_count + count - 2
    else:
        for hop in (1, -1, 2, -2):
            friend = me + hop
            there = jnp.logical_and(friend >= 0, friend < count)

            @pl.when(there)
            def _():
                pl.semaphore_signal(
                    barrier, 1, device_id={"ctx": friend}, device_id_type=MESH
                )

            friends = friends + there.astype(jnp.int32)
    lax.fori_loop(0, blocks, build_masks, 0)
    for tap in range(1, taps):
        mask_scr[tap - 1] = jnp.where(
            offx_ref[tap : tap + tok + SUB, :] >= float(tap), 1.0, 0.0
        )
    dev_ref[...] = jnp.where(
        jnp.broadcast_to(offx_ref[SUB + tok - 1 : SUB + tok, :], (SUB, LANES)) >= float(tok),
        1.0,
        0.0,
    )

    def pack(chunk, carry):
        cols = pl.ds(pl.multiple_of(chunk * width, width), width)
        for branch, ref in enumerate(sources):
            edge_scr[...] = ref[tok - 2 * SUB : tok, cols].astype(F32)
            pack_scr[branch * rim : (branch + 1) * rim, :] = edge_scr[2 * SUB - rim :, :]
        rim_send[chunk] = pack_scr[...].astype(BF16)
        return carry

    pack_scr[...] = jnp.zeros(pack_scr.shape, F32)
    lax.fori_loop(0, chunks, pack, 0)
    pl.semaphore_wait(barrier, friends)

    def remote(source, target, send, recv, device):
        return pltpu.make_async_remote_copy(
            src_ref=source,
            dst_ref=target,
            send_sem=send,
            recv_sem=recv,
            device_id=device,
            device_id_type=MESH,
        )

    def chunk_cols(chunk):
        return pl.ds(pl.multiple_of(chunk * width, width), width)

    def tile_cols(chunk, step):
        return pl.ds(pl.multiple_of(chunk * width + step * LANES, LANES), LANES)

    def lane_cols(step):
        return pl.ds(pl.multiple_of(step * LANES, LANES), LANES)

    def rim_copy(chunk):
        return remote(
            rim_send.at[chunk],
            rim_recv.at[chunk],
            rim_s.at[chunk],
            rim_r.at[chunk],
            {"ctx": me + 1},
        )

    def pair_copy(chunk):
        return remote(
            ends.at[1 - odd, chunk],
            pair_recv.at[chunk],
            pair_s.at[chunk],
            pair_r.at[chunk],
            {"ctx": partner},
        )

    def chain_copy(chunk):
        return remote(
            chain_out.at[chunk],
            chain_recv.at[odd, chunk],
            ea_s.at[chunk],
            ea_r.at[chunk],
            {"ctx": me + 2 * lead},
        )

    def cross_copy(chunk):
        return remote(
            chain_out.at[chunk],
            chain_recv.at[odd, chunk],
            eb_s.at[chunk],
            eb_r.at[chunk],
            {"ctx": me + lead},
        )

    def cross_arrival(chunk):
        return remote(
            chain_out.at[chunk],
            chain_recv.at[1 - odd, chunk],
            eb_s.at[chunk],
            eb_r.at[chunk],
            {"ctx": me - lead},
        )

    def head_copy(chunk):
        return remote(
            head_send.at[chunk],
            head_recv.at[chunk],
            head_s.at[chunk],
            head_r.at[chunk],
            {"ctx": me - 1},
        )

    flag_copy = remote(dev_ref, flag_recv, flag_s, flag_r, {"ctx": partner})
    flag_copy.start()

    @pl.when(me + 1 < count)
    def _():
        def send(chunk, carry):
            rim_copy(chunk).start()
            return carry

        lax.fori_loop(0, chunks, send, 0)

    @pl.when(me == 0)
    def _():
        rim_recv[...] = jnp.zeros(rim_recv.shape, BF16)

    @pl.when(place == 0)
    def _():
        chain_recv[odd] = jnp.zeros(chain_recv.shape[1:], F32)

    @pl.when(other_place == 0)
    def _():
        chain_recv[1 - odd] = jnp.zeros(chain_recv.shape[1:], F32)

    def fill(branch, chunk, step, cols):
        if branch == 0:
            rim_scr[...] = rim_recv[chunk, :, lane_cols(step)].astype(F32)
        ext_ref[branch, 0:SUB, :] = jnp.zeros((SUB, LANES), F32)
        ext_ref[branch, SUB - rim : SUB, :] = rim_scr[branch * rim : (branch + 1) * rim, :]
        source = sources[branch][:, cols].astype(F32)
        ext_ref[branch, SUB:, :] = source
        return source

    def local_tile(chunk, step):
        cols = tile_cols(chunk, step)
        offs = offx_ref[SUB : SUB + tok, :]
        outs = []
        for branch, out in enumerate((qs_scr, ks_scr, vs_scr)):
            source = fill(branch, chunk, step, cols)
            total = short_ref[branch, 0:1, cols] * source
            for tap in range(1, taps):
                window = ext_ref[branch, SUB - tap : SUB - tap + tok, :]
                total = total + short_ref[branch, tap : tap + 1, cols] * jnp.where(
                    offs >= float(tap), window, 0.0
                )
            out[:, cols] = total
            outs.append(total)
        xm_ref[...] = outs[1] * outs[2] * last_ref[...]
        zm_ref[...] = og_ref[:, cols].astype(F32) * outs[0] * valid_ref[...]
        lam = jnp.exp(lamlog_ref[:, cols])
        powers = decay_powers(lam)
        span = powers[SUB - 1] * lam

        def sub_block(block, state):
            total, adjoint, weight = state
            base = block * SUB
            sigma = xm_ref[pl.ds(base + SUB - 1, 1), :] * powers[0]
            gamma = zm_ref[pl.ds(base, 1), :] * powers[0]
            for pos in range(1, SUB):
                sigma = sigma + powers[pos] * xm_ref[pl.ds(base + SUB - 1 - pos, 1), :]
                gamma = gamma + powers[pos] * zm_ref[pl.ds(base + pos, 1), :]
            sig_scr[block, :, cols] = sigma
            gam_scr[block, :, cols] = gamma
            factor = span * pass_ref[pl.ds(block, 1), :]
            return (sigma + factor * total, adjoint + weight * gamma, weight * factor)

        zero = jnp.zeros_like(lam)
        total, adjoint, _ = lax.fori_loop(
            0, blocks, sub_block, (zero, zero, jnp.ones_like(lam)), unroll=8
        )
        ends[1, chunk, :, lane_cols(step)] = total
        ends[0, chunk, :, lane_cols(step)] = adjoint

    def chain_tile(chunk, step):
        at = lane_cols(step)
        decay = jnp.exp(float(tok) * lamlog_ref[:, tile_cols(chunk, step)])
        state = (
            pair_recv[chunk, :, at]
            + decay * flag_recv[0:1, :] * chain_recv[odd, chunk, :, at]
        )
        chain_recv[odd, chunk, :, at] = state
        chain_out[chunk, :, at] = ends[odd, chunk, :, at] + decay * dev_ref[0:1, :] * state

    def main_tile(chunk, step):
        cols = tile_cols(chunk, step)
        at_lanes = lane_cols(step)
        lamlog = lamlog_ref[:, cols]
        coef = coef_ref[:, cols]
        lam = jnp.exp(lamlog)
        powers = decay_powers(lam)
        span = powers[SUB - 1] * lam
        for lag in range(SUB):
            filt_scr[lag : lag + 1, :] = jnp.sum(coef * powers[lag], axis=0, keepdims=True)
        for mode in range(modes):
            log_row = lamlog[mode : mode + 1, :]
            coef_row = coef[mode : mode + 1, :]
            fwd_scr[mode] = coef_row * jnp.exp(log_row * (rows + 1.0))
            bwd_scr[mode] = coef_row * jnp.exp(log_row * (float(SUB) - rows))

        def sweep(index, state):
            forward, backward = state
            back = blocks - 1 - index
            enters_scr[index] = forward
            exits_scr[back] = backward
            forward = sig_scr[index, :, cols] + span * pass_ref[pl.ds(index, 1), :] * forward
            backward = gam_scr[back, :, cols] + span * pass_ref[pl.ds(back, 1), :] * backward
            return forward, backward

        lax.fori_loop(
            0,
            blocks,
            sweep,
            (chain_recv[1, chunk, :, at_lanes], chain_recv[0, chunk, :, at_lanes]),
            unroll=8,
        )

        for branch in range(3):
            fill(branch, chunk, step, cols)
            g_ref[branch, 0:SUB, :] = jnp.zeros((SUB, LANES), F32)
            g_ref[branch, SUB + tok :, :] = jnp.zeros((SUB, LANES), F32)
        xm_ref[...] = og_ref[:, cols].astype(F32)
        skip = skip_ref[:, cols]

        def sub_block(block, state):
            lag_sums, res = state
            at = pl.ds(pl.multiple_of(block * SUB, SUB), SUB)
            query = qs_scr[at, cols]
            key = ks_scr[at, cols]
            value = vs_scr[at, cols]
            grad = xm_ref[at, :]
            mixed = key * value
            z_grad = grad * query
            offin = offin_ref[at, :]
            cross = jnp.zeros((SUB, LANES), F32)
            cross_back = jnp.zeros((SUB, LANES), F32)
            for mode in range(modes):
                cross = cross + fwd_scr[mode] * enters_scr[block, mode : mode + 1, :]
                cross_back = cross_back + bwd_scr[mode] * exits_scr[block, mode : mode + 1, :]
            first = filt_scr[0:1, :]
            forward = valid_ref[at, :] * cross + (first + skip) * mixed
            backward = last_ref[at, :] * cross_back + (first + skip) * z_grad
            new_sums = [lag_sums[0] + z_grad * mixed]
            for lag in range(1, SUB):
                inside = offin >= float(lag)
                tap = filt_scr[lag : lag + 1, :]
                shifted = jnp.where(inside, pltpu.roll(mixed, lag, 0), 0.0)
                forward = forward + tap * shifted
                new_sums.append(lag_sums[lag] + z_grad * shifted)
                backward = backward + tap * pltpu.roll(
                    jnp.where(inside, z_grad, 0.0), SUB - lag, 0
                )
            res = res + gam_scr[block, :, cols] * enters_scr[block]
            xm_ref[at, :] = query * forward
            put = pl.ds(pl.multiple_of(block * SUB + SUB, SUB), SUB)
            g_ref[0, put, :] = grad * forward
            g_ref[1, put, :] = backward * value
            g_ref[2, put, :] = backward * key
            return tuple(new_sums), res

        lag_sums, res = lax.fori_loop(
            0,
            blocks,
            sub_block,
            (
                tuple(jnp.zeros((SUB, LANES), F32) for _ in range(SUB)),
                jnp.zeros((modes, LANES), F32),
            ),
            unroll=8,
        )
        mo_ref[:, cols] = xm_ref[...].astype(BF16)
        res = res * lam
        sums = [jnp.sum(lag_sum, axis=0, keepdims=True) for lag_sum in lag_sums]
        for lag in range(SUB):
            res = res + powers[lag] * sums[lag]
        skip_row = 3 * taps
        res_row = acc.shape[1] - modes
        acc[chunk, skip_row:res_row, at_lanes] = jnp.concatenate(
            [sums[0], jnp.zeros((res_row - skip_row - 1, LANES), F32)], axis=0
        )
        acc[chunk, res_row:, at_lanes] = norm_ref[:, cols] * res

        span_rows = tok + SUB
        for branch, out in enumerate((qg_ref, kg_ref, vg_ref)):
            source = ext_ref[branch]
            spread = jnp.zeros((span_rows, LANES), F32)
            for tap in range(taps):
                moved = g_ref[branch, tap : tap + span_rows, :]
                if tap > 0:
                    moved = moved * mask_scr[tap - 1]
                spread = spread + short_ref[branch, tap : tap + 1, cols] * moved
                row = branch * taps + tap
                acc[chunk, row : row + 1, at_lanes] = jnp.sum(
                    source * moved, axis=0, keepdims=True
                )
            head_send[chunk, branch, :, at_lanes] = spread[0:SUB, :]
            out[:, cols] = spread[SUB:, :].astype(BF16)
            tail_scr[chunk, branch, :, at_lanes] = spread[span_rows - 2 * SUB :, :]

    def each_tile(work, chunk):
        def one(step, carry):
            work(chunk, step)
            return carry

        lax.fori_loop(0, tiles, one, 0)

    def dp_copy(chunk, step):
        peer = (dp + step) % dp_count
        return remote(
            acc.at[chunk, :, lane_cols(peer)],
            dp_recv.at[chunk, step - 1],
            s1.at[chunk, step - 1],
            r1.at[chunk, step - 1],
            {"dp": peer},
        )

    def owner_of(chunk):
        return (chunk + count // 2) % count

    my_chunk = (me + count - count // 2) % count

    def ctx_copy(chunk):
        owner = owner_of(chunk)
        slot = (me - owner + count) % count - 1
        return remote(
            part.at[chunk], ctx_recv.at[slot], s2.at[chunk], r2.at[slot], {"ctx": owner}
        )

    def ctx_arrival(slot):
        return remote(
            part.at[0], ctx_recv.at[slot], s2.at[0], r2.at[slot], {"ctx": partner}
        )

    def gather_copy(chunk, step):
        place_cols = tile_cols(chunk, dp)
        return remote(
            full.at[:, place_cols],
            full.at[:, place_cols],
            s3.at[step - 1],
            r3.at[chunk],
            {"ctx": (me + step) % count},
        )

    def forward_copy(chunk, step):
        place_cols = tile_cols(chunk, dp)
        return remote(
            full.at[:, place_cols],
            full.at[:, place_cols],
            s4.at[chunk, step - 1],
            r4.at[chunk, step - 1],
            {"dp": (dp + step) % dp_count},
        )

    def forward_arrival(chunk, step):
        place_cols = tile_cols(chunk, (dp + dp_count - step) % dp_count)
        return remote(
            full.at[:, place_cols],
            full.at[:, place_cols],
            s4.at[chunk, step - 1],
            r4.at[chunk, step - 1],
            {"dp": (dp + step) % dp_count},
        )

    def sum_parts(done):
        total = acc[done, :, lane_cols(dp)]
        for step in range(1, dp_count):
            dp_copy(done, step).wait_recv()
            total = total + dp_recv[done, step - 1]
        part[done] = total

        @pl.when(owner_of(done) != me)
        def _():
            ctx_copy(done).start()

    flag_copy.wait()

    def slot_body(slot, carry):
        @pl.when(slot < chunks)
        def _():
            @pl.when(me > 0)
            def _():
                rim_copy(slot).wait_recv()

            each_tile(local_tile, slot)
            pair_copy(slot).start()

        link = slot - 3 - (5 * place) // 3

        @pl.when(jnp.logical_and(link >= 0, link < chunks))
        def _():
            pair_copy(link).wait_recv()

            @pl.when(place > 0)
            def _():
                chain_copy(link).wait_recv()

            each_tile(chain_tile, link)

            @pl.when(place < pairs - 1)
            def _():
                chain_copy(link).start()
                cross_copy(link).start()

        now = slot - first_main

        @pl.when(jnp.logical_and(now >= 0, now < chunks))
        def _():
            @pl.when(other_place > 0)
            def _():
                cross_arrival(now).wait_recv()

            def one(step, inner):
                if fused:

                    @pl.when(jnp.logical_and(step == tiles // 2, now > 0))
                    def _():
                        sum_parts(now - 1)

                main_tile(now, step)
                return inner

            lax.fori_loop(0, tiles, one, 0)

            @pl.when(me > 0)
            def _():
                head_copy(now).start()

            if fused:
                for step in range(1, dp_count):
                    dp_copy(now, step).start()

        done = now - 1

        @pl.when(jnp.logical_and(done >= 0, done < chunks))
        def _():
            if fused:

                @pl.when(done == chunks - 1)
                def _():
                    sum_parts(chunks - 1)

            @pl.when(me + 1 < count)
            def _():
                head_copy(done).wait_recv()
                for branch, out in enumerate((qg_ref, kg_ref, vg_ref)):
                    tail = tail_scr[done, branch]
                    tail = jnp.concatenate(
                        [tail[0:SUB, :], tail[SUB:, :] + head_recv[done, branch]], axis=0
                    )
                    out[tok - 2 * SUB : tok, chunk_cols(done)] = tail.astype(BF16)

        if fused:

            @pl.when(done == my_chunk)
            def _():
                total = part[my_chunk]
                for index in range(count - 1):
                    ctx_arrival(index).wait_recv()
                    total = total + ctx_recv[index]
                full[:, tile_cols(my_chunk, dp)] = total * scale
                for step in range(1, count):
                    gather_copy(my_chunk, step).start()

            ready = now - 2

            @pl.when(jnp.logical_and(ready >= 0, ready < chunks))
            def _():
                @pl.when(ready != my_chunk)
                def _():
                    gather_copy(ready, 1).wait_recv()

                for step in range(1, dp_count):
                    forward_copy(ready, step).start()

        return carry

    lax.fori_loop(0, first_main + chunks + 2, slot_body, 0)

    if fused:

        def arrive(chunk, carry):
            for step in range(1, dp_count):
                forward_arrival(chunk, step).wait_recv()
            return carry

        lax.fori_loop(0, chunks, arrive, 0)

    def emit(chunk, carry):
        cols = chunk_cols(chunk)
        sums = full[:, cols] if fused else acc[chunk]
        for branch in range(3):
            taps_out[branch, :, cols] = sums[branch * taps : (branch + 1) * taps, :]
        skip_out[:, cols] = sums[3 * taps : 3 * taps + 1, :]
        res_out[:, cols] = sums[sums.shape[0] - modes :, :]
        return carry

    lax.fori_loop(0, chunks, emit, 0)

    def drain(chunk, carry):
        pair_copy(chunk).wait_send()

        @pl.when(me + 1 < count)
        def _():
            rim_copy(chunk).wait_send()

        @pl.when(place < pairs - 1)
        def _():
            chain_copy(chunk).wait_send()
            cross_copy(chunk).wait_send()

        @pl.when(me > 0)
        def _():
            head_copy(chunk).wait_send()

        if fused:
            for step in range(1, dp_count):
                dp_copy(chunk, step).wait_send()

                forward_copy(chunk, step).wait_send()

            @pl.when(owner_of(chunk) != me)
            def _():
                ctx_copy(chunk).wait_send()

        return carry

    lax.fori_loop(0, chunks, drain, 0)
    if fused:
        for step in range(1, count):
            gather_copy(my_chunk, step).wait_send()


def settle_kernel(*refs):
    half = len(refs) // 2
    for source, target in zip(refs[:half], refs[half:]):
        target[...] = source[...]


def settle(arrays):
    channels = arrays[0].shape[-1]
    width = channels // 4

    def spec(array):
        zeros = (0,) * (array.ndim - 1)
        return pl.BlockSpec(array.shape[:-1] + (width,), lambda i: zeros + (i,))

    return pl.pallas_call(
        settle_kernel,
        grid=(4,),
        out_shape=[jax.ShapeDtypeStruct(a.shape, a.dtype) for a in arrays],
        in_specs=[spec(a) for a in arrays],
        out_specs=[spec(a) for a in arrays],
        compiler_params=pltpu.CompilerParams(
            dimension_semantics=("arbitrary",), vmem_limit_bytes=56 << 20
        ),
        name="settle_outputs",
    )(*arrays)


def shards(
    query_proj,
    key_proj,
    value_proj,
    doc_offset,
    short_taps,
    rate_scale,
    residue,
    skip_gain,
    out_grad,
):
    row_count, tok, channels = query_proj.shape
    count = lax.axis_size("ctx")
    dp_count = lax.axis_size("dp")
    seq_len = tok * count
    scale = 1.0 / math.sqrt(row_count * dp_count * seq_len)
    taps = short_taps.shape[1]
    modes = rate_scale.shape[0]
    blocks = tok // SUB
    fused = channels == dp_count * count * LANES
    width = dp_count * LANES if fused else 4 * LANES
    chunks = channels // width

    lam_log = -rate_scale / seq_len
    norm = jnp.sqrt(-jnp.expm1(2.0 * lam_log))
    coef = residue * norm

    offs = jnp.pad(doc_offset[0], (SUB, SUB)).astype(F32)
    offs_ext = jnp.broadcast_to(offs[:, None], (tok + 2 * SUB, LANES))

    acc_rows = -(-(3 * taps + 1) // SUB) * SUB + modes
    dma = pltpu.SemaphoreType.DMA
    vmem = pl.BlockSpec(memory_space=pltpu.VMEM)
    dp_steps, ctx_steps = max(dp_count - 1, 1), max(count - 1, 1)
    rim_rows = -(-3 * (taps - 1) // (2 * SUB)) * 2 * SUB

    def scr(*dims, dtype=F32):
        return pltpu.VMEM(dims, dtype)

    outs = pl.pallas_call(
        functools.partial(fused_kernel, (taps, width, dp_count, count, fused, scale)),
        out_shape=[jax.ShapeDtypeStruct((tok, channels), BF16)] * 4
        + [
            jax.ShapeDtypeStruct((3, taps, channels), F32),
            jax.ShapeDtypeStruct((1, channels), F32),
            jax.ShapeDtypeStruct((modes, channels), F32),
        ],
        in_specs=[vmem] * 10,
        out_specs=[vmem] * 7,
        scratch_shapes=[scr(tok, channels)] * 3
        + [scr(blocks, modes, channels)] * 2
        + [
            scr(tok, LANES),
            scr(tok, LANES),
            scr(tok, LANES),
            scr(blocks, LANES),
            scr(SUB, LANES),
            scr(taps - 1, tok + SUB, LANES),
            scr(2 * SUB, width),
            scr(rim_rows, width),
            scr(rim_rows, LANES),
            scr(chunks, rim_rows, width, dtype=BF16),
            scr(chunks, rim_rows, width, dtype=BF16),
            scr(2, chunks, modes, width),
            scr(chunks, modes, width),
            scr(chunks, modes, width),
            scr(2, chunks, modes, width),
            scr(SUB, LANES),
            scr(chunks, 3, SUB, width),
            scr(chunks, 3, SUB, width),
            scr(chunks, 3, 2 * SUB, width),
            scr(chunks, acc_rows, width),
            scr(chunks, dp_steps, acc_rows, LANES),
            scr(chunks, acc_rows, LANES),
            scr(ctx_steps, acc_rows, LANES),
            scr(acc_rows, channels),
            scr(3, SUB + tok, LANES),
            scr(3, tok + 2 * SUB, LANES),
            scr(tok, LANES),
            scr(tok, LANES),
            scr(blocks, modes, LANES),
            scr(blocks, modes, LANES),
            scr(modes, SUB, LANES),
            scr(modes, SUB, LANES),
            scr(SUB, LANES),
            dma,
            dma,
        ]
        + [dma((chunks,))] * 10
        + [dma((chunks, dp_steps))] * 2
        + [dma((chunks,)), dma((ctx_steps,))]
        + [dma((ctx_steps,)), dma((chunks,))]
        + [dma((chunks, dp_steps))] * 2,
        compiler_params=pltpu.CompilerParams(
            collective_id=0, has_side_effects=True, vmem_limit_bytes=56 << 20
        ),
        name="hyena_fused",
    )(
        query_proj[0],
        key_proj[0],
        value_proj[0],
        out_grad[0],
        offs_ext,
        short_taps,
        lam_log,
        coef,
        norm,
        skip_gain[None, :],
    )
    outs = settle(outs)
    sums = (outs[4], outs[5][0], outs[6])
    if not fused:
        sums = tuple(s * scale for s in lax.psum(sums, ("dp", "ctx")))
    return tuple(o[None] for o in outs[:4]) + sums


def solution(mesh):
    tokens = P("dp", "ctx", None)
    in_specs = (tokens, tokens, tokens, P("dp", "ctx"), P(), P(), P(), P(), tokens)
    out_specs = (tokens, tokens, tokens, tokens, P(), P(), P())
    return jax.shard_map(shards, mesh=mesh, in_specs=in_specs, out_specs=out_specs, check_vma=False)
```
